128 devices in a mesh: row: 16 (over y_hi, z, core), col: 4 (over x), gz: 2 (over y_lo).
Axes of the slice: x: 4, y: 4 (y_hi: 2, y_lo: 2; y = y_hi * 2 + y_lo), z: 4, core: 2. Of those that a mesh axis runs over, the one named last changes fastest.
Arguments:
- velocity_hat: bfloat16 [3, 2, 2, 4096, 4096], P(None, None, 'gz', ('row', 'col')), may hold values from -6 to 6
Outputs:
- smoothed: float32 [2, 4096, 4096], P('gz', 'col', 'row')
The draws below stay inside these ranges and needn't reach their ends.
All inputs are finite; a program needn't handle non-finite values.
Results may differ from the reference program's by a relative error of at most 0.002.
Values may be sent and summed in bfloat16 or wider, within the bound.
No kernel may reach another device: no remote copies, remote signals or barrier semaphores. Data moves between devices by JAX's collectives and lax.ppermute only.
A program may use at most 128 MiB of HBM per device.

```python
import math
import jax
import jax.numpy as jnp
from jax import lax

GRID = 4096
PLANES = 2


def steps_of(rng, dims, cuts, least, high):
    def one(dim, blocks):
        heights = jax.random.uniform(jax.random.fold_in(jax.random.fold_in(rng, 6), dim), (blocks,), jnp.float32, least / len(cuts), high / len(cuts))
        return jnp.repeat(jnp.exp(heights), dims[dim] // blocks).reshape((-1,) + (1,) * (len(dims) - dim - 1))

    factor_of = one(*cuts[0])
    for cut in cuts[1:]:
        factor_of = factor_of * one(*cut)
    return factor_of


def centred(rng, dims, deviation, most, split=(), kind=jnp.bfloat16):
    factor_of = steps_of(rng, dims, split, -0.22, 0.18) if split else 1.0
    result = jax.random.normal(rng, dims, jnp.float32) * deviation * factor_of
    return jnp.minimum(jnp.maximum(result, -most), most).astype(kind)


def setup_inputs(seed: int = 0) -> dict:
    keys = jax.random.split(jax.random.key(seed), 2)
    velocity_hat = centred(keys[0], (3, 2, PLANES, GRID, GRID), 1.0, 6.0, ((2, 2), (3, 64)))
    return {"velocity_hat": velocity_hat}


relax_weight = 0.15

def wavenumber(index, length):
    signed = (index + length // 2) % length - length // 2
    return signed.astype(jnp.float32) * (2.0 * math.pi / length)

def plane_step(field):
    return jnp.roll(field, -1, 0) - field

def smooth_pass(field):
    beside_all = jnp.roll(field, 1, 0) + jnp.roll(field, -1, 0)
    beside_all = beside_all + jnp.roll(field, 1, 1) + jnp.roll(field, -1, 1)
    beside_all = beside_all + jnp.roll(field, 1, 2) + jnp.roll(field, -1, 2)
    return field + relax_weight * (beside_all - 6.0 * field)

def reference(velocity_hat):
    parts = velocity_hat.astype(jnp.float32)
    wave_x = wavenumber(jnp.arange(GRID, dtype=jnp.int32), GRID)[None, None, :]
    wave_y = wavenumber(jnp.arange(GRID, dtype=jnp.int32), GRID)[None, :, None]

    def spectral(which):
        return lax.complex(parts[which, 0], parts[which, 1])

    def vort_hat(which):
        along_x = spectral(0)
        along_y = spectral(1)
        along_z = spectral(2)
        if which == 0:
            return 1j * wave_y * along_z - plane_step(along_y)
        if which == 1:
            return plane_step(along_x) - 1j * wave_x * along_z
        return 1j * (wave_x * along_y - wave_y * along_x)
    total = jnp.ones(parts.shape[2:], jnp.float32)
    for which in range(3):
        vort = jnp.real(jnp.fft.ifft2(vort_hat(which), norm='ortho')).astype(jnp.float32)
        total = total + vort * vort
    field = jnp.sqrt(total)
    for pass_index in range(3):
        field = smooth_pass(field)
    return field
```

```python
import math

import jax
import jax.numpy as jnp
import numpy as np
from jax import lax
from jax.experimental import pallas as pl
from jax.experimental.pallas import tpu as pltpu
from jax.sharding import PartitionSpec as P

GRID = 4096
RELAX = 0.15
VMEM_LIMIT = 48 * 1024 * 1024
NT = (((1,), (1,)), ((), ()))


def split_bf16(table):
    high = table.astype(jnp.bfloat16)
    low = (table - high.astype(np.float64)).astype(jnp.bfloat16)
    return np.concatenate([high, low], axis=0)


def tables():
    k = np.arange(128)
    blocks = []
    for s in range(2):
        angle = 2 * np.pi * ((np.arange(64)[:, None] * 2 + s) * k[None, :] % 128) / 128
        c, d = np.cos(angle), np.sin(angle)
        blocks.append(np.concatenate([c, -d], axis=1))
        blocks.append(np.concatenate([d, c], axis=1))
    x_matrix = split_bf16(np.concatenate(blocks, axis=0))
    angle = 2 * np.pi * (np.arange(32)[:, None] * k[None, :]) / 4096
    x_twist = np.stack([np.cos(angle), np.sin(angle)]).astype(np.float32) / 64
    j = np.arange(64)
    angle = 2 * np.pi * (j[:, None] * j[None, :] % 64) / 64
    zero = np.zeros((64, 64))
    c, d = np.cos(angle), -np.sin(angle)
    y_matrix = split_bf16(
        np.concatenate(
            [np.concatenate([c, zero, d, zero], axis=1), np.concatenate([zero, c, zero, d], axis=1)], axis=0
        )
    )
    angle = 2 * np.pi * (j[:, None] * j[None, :]) / 4096
    y_twist = np.stack([np.cos(angle), np.sin(angle)]).astype(np.float32) / 64
    y_twist = np.concatenate([y_twist, y_twist], axis=2)
    return x_matrix, x_twist, y_matrix, y_twist


def turned(value, num, den):
    re, im = value
    num = num % den
    if num == 0:
        return value
    if 2 * num == den:
        return (-re, -im)
    if 4 * num == den:
        return (-im, re)
    if 4 * num == 3 * den:
        return (im, -re)
    if 8 * num == den:
        r = math.sqrt(0.5)
        return ((re - im) * r, (re + im) * r)
    if 8 * num == 3 * den:
        r = math.sqrt(0.5)
        return ((re + im) * -r, (re - im) * r)
    c, s = math.cos(2 * math.pi * num / den), math.sin(2 * math.pi * num / den)
    return (re * c - im * s, re * s + im * c)


def plus(a, b):
    return (a[0] + b[0], a[1] + b[1])


def minus(a, b):
    return (a[0] - b[0], a[1] - b[1])


def dft4(v):
    a, b = plus(v[0], v[2]), minus(v[0], v[2])
    c, d = plus(v[1], v[3]), minus(v[1], v[3])
    return [plus(a, c), (b[0] - d[1], b[1] + d[0]), minus(a, c), (b[0] + d[1], b[1] - d[0])]


def dft8(v):
    even, odd = dft4(v[0::2]), dft4(v[1::2])
    odd = [turned(odd[t], t, 8) for t in range(4)]
    return [plus(e, o) for e, o in zip(even, odd)] + [minus(e, o) for e, o in zip(even, odd)]


def x_kernel(which, rows_local, *refs):
    n_in = 2 if which == 2 else 3
    ins, (matrix, twist, out, stage, lines, spread) = refs[:n_in], refs[n_in:]
    step = pl.program_id(0)
    scale = 2.0 * math.pi / GRID
    lane = lax.broadcasted_iota(jnp.int32, (16, 128), 1)
    row = lax.broadcasted_iota(jnp.int32, (16, 128), 0)
    start = lax.axis_index(("row", "col")) * rows_local + step * 16
    ky = row + start
    wave_y = jnp.where(ky >= GRID // 2, ky - GRID, ky).astype(jnp.float32) * scale

    def tile(ref, part, q):
        return ref[0, part, :, pl.ds(q * 128, 128)].astype(jnp.float32)

    def wave_x(q):
        base = q * 128 - (GRID if q >= 16 else 0)
        return (lane + base).astype(jnp.float32) * scale

    def curl(q):
        if which == 2:
            u, v = ins
            wx = wave_x(q)
            return (
                wave_y * tile(u, 1, q) - wx * tile(v, 1, q),
                wx * tile(v, 0, q) - wave_y * tile(u, 0, q),
            )
        w, f, g = ins
        step_re = tile(g, 0, q) - tile(f, 0, q)
        step_im = tile(g, 1, q) - tile(f, 1, q)
        if which == 0:
            return (-wave_y * tile(w, 1, q) - step_re, wave_y * tile(w, 0, q) - step_im)
        wx = wave_x(q)
        return (step_re + wx * tile(w, 1, q), step_im - wx * tile(w, 0, q))

    for a in range(8):
        for b, value in enumerate(dft4([curl(a + 8 * t) for t in range(4)])):
            value = turned(value, a * b, 32)
            stage[0, b * 8 + a] = value[0]
            stage[1, b * 8 + a] = value[1]
    for b in range(4):
        for t, value in enumerate(dft8([(stage[0, b * 8 + a], stage[1, b * 8 + a]) for a in range(8)])):
            n = b + 4 * t
            c, s = twist[0, n : n + 1, :], twist[1, n : n + 1, :]
            at = pl.ds(((n % 16) * 2 + n // 16) * 64 + step * 16, 16)
            lines[at, 0:128] = (value[0] * c - value[1] * s).astype(jnp.bfloat16)
            lines[at, 128:256] = (value[0] * s + value[1] * c).astype(jnp.bfloat16)

    @pl.when(step == 3)
    def _():
        for pair in range(8):
            got = lax.dot_general(
                matrix[...], lines[pl.ds(pair * 256, 256), :], NT, preferred_element_type=jnp.float32
            )
            got = got[0:256] + got[256:512]
            for half in range(2):
                n16 = pair * 2 + half
                for s in range(2):
                    for c in range(2):
                        at = (s * 2 + c) * 64
                        spread[pl.ds(c * 32 + s * 16 + n16, 64, stride=64), :] = got[
                            at : at + 64, half * 128 : half * 128 + 128
                        ]
        for b in range(64):
            out[b] = spread[pl.ds(b * 64, 64), :].astype(jnp.bfloat16)


def x_transform(which, fields, x_matrix, x_twist):
    rows_local = fields[0][0].shape[2]
    specs = [
        pl.BlockSpec((1, 2, 16, GRID), lambda i, comp=comp: (comp, 0, i, 0)) for _, comp in fields
    ] + [
        pl.BlockSpec((512, 256), lambda i: (0, 0)),
        pl.BlockSpec((2, 32, 128), lambda i: (0, 0, 0)),
    ]
    return pl.pallas_call(
        lambda *refs: x_kernel(which, rows_local, *refs),
        grid=(rows_local // 16,),
        in_specs=specs,
        out_specs=pl.BlockSpec((64, 64, 128), lambda i: (0, 0, 0)),
        out_shape=jax.ShapeDtypeStruct((64, 64, 128), jnp.bfloat16),
        scratch_shapes=[
            pltpu.VMEM((2, 32, 16, 128), jnp.float32),
            pltpu.VMEM((2048, 256), jnp.bfloat16),
            pltpu.VMEM((4096, 128), jnp.float32),
        ],
        compiler_params=pltpu.CompilerParams(vmem_limit_bytes=VMEM_LIMIT),
        name=f"curl_x_{which}",
    )(*[array for array, _ in fields], x_matrix, x_twist)


def y_lines(source, twist, stage, lines):
    def one(part, carry):
        def load(c, d):
            return source[d, pl.ds(c * 32 + part * 16, 16), :].astype(jnp.float32)

        for a in range(8):
            values = [(load(0, a + 8 * t), load(1, a + 8 * t)) for t in range(8)]
            for b, value in enumerate(dft8(values)):
                value = turned(value, a * b, 64)
                stage[0, b * 8 + a] = value[0]
                stage[1, b * 8 + a] = value[1]
        for b in range(8):
            for t, value in enumerate(dft8([(stage[0, b * 8 + a], stage[1, b * 8 + a]) for a in range(8)])):
                n = b + 8 * t
                c, s = twist[0, n : n + 1, :], twist[1, n : n + 1, :]
                at = pl.ds(n * 32 + part * 16, 16)
                lines[at, 0:128] = (value[0] * c - value[1] * s).astype(jnp.bfloat16)
                lines[at, 128:256] = (value[0] * s + value[1] * c).astype(jnp.bfloat16)
        return carry

    lax.fori_loop(0, 2, one, 0)


def y_kernel(*refs):
    sources, (matrix, twist, out, stage, lines, total) = refs[:3], refs[3:]
    for index, source in enumerate(sources):
        y_lines(source, twist, stage, lines)
        for chunk in range(8):
            got = lax.dot_general(
                matrix[...], lines[pl.ds(chunk * 256, 256), :], NT, preferred_element_type=jnp.float32
            )
            got = got[0:128] + got[128:256]
            at = (slice(None), slice(chunk * 256, chunk * 256 + 256))
            if index == 0:
                total[at] = 1.0 + got * got
            elif index == 1:
                total[at] = total[at] + got * got
            else:
                total[at] = jnp.sqrt(total[at] + got * got)

    def put(h, tile, value):
        value = value.astype(jnp.bfloat16)
        for c in range(4):
            for z in range(2):
                out[z * 4 + c, h * 16 : h * 16 + 16, tile * 128 : tile * 128 + 128] = value[c * 16 : c * 16 + 16]

    for h in range(2):
        rows = slice(h * 64, h * 64 + 64)
        for tile in range(16):
            put(h, tile + 1, total[rows, tile * 128 : tile * 128 + 128])
        put(h, 0, pltpu.roll(total[rows, 15 * 128 : 16 * 128], 1, 0))
        put(h, 17, pltpu.roll(total[rows, 0:128], 63, 0))


def y_transform(sources, y_matrix, y_twist):
    return pl.pallas_call(
        y_kernel,
        out_shape=jax.ShapeDtypeStruct((8, 32, 2304), jnp.bfloat16),
        scratch_shapes=[
            pltpu.VMEM((2, 64, 16, 128), jnp.float32),
            pltpu.VMEM((2048, 256), jnp.bfloat16),
            pltpu.VMEM((128, 2048), jnp.float32),
        ],
        compiler_params=pltpu.CompilerParams(vmem_limit_bytes=VMEM_LIMIT),
        name="y_magnitude",
    )(*sources, y_matrix, y_twist)


def smooth_coefficients():
    w = RELAX
    even = np.polynomial.polynomial.polypow([1 - 6 * w + 2 * w, w], 3)
    odd = np.polynomial.polynomial.polypow([1 - 6 * w - 2 * w, w], 3)
    return (even + odd) / 2, (even - odd) / 2


def smooth_kernel(field, low, high, out, own, other, work, spread):
    own_c, other_c = [[float(v) for v in part] for part in smooth_coefficients()]
    me = lax.axis_index("gz")
    lane = lax.broadcasted_iota(jnp.int32, (16, 128), 1)

    def swapped(a, b, width):
        upper = (lane & width) != 0
        return (
            jnp.where(upper, pltpu.roll(b, width, 1), a),
            jnp.where(upper, b, pltpu.roll(a, 128 - width, 1)),
        )

    def gather(z, target, tile):
        at = pl.ds(pl.multiple_of(tile * 128, 128), 128)
        v = {
            (c, h): field[z * 4 + c, h * 16 : h * 16 + 16, at].astype(jnp.float32)
            for c in range(4)
            for h in range(2)
        }
        edge_low = low[z, :, at].astype(jnp.float32)
        edge_high = high[z, :, at].astype(jnp.float32)
        for ch in range(2):
            p = {}
            for h in range(2):
                p[0, h], p[1, h] = swapped(v[ch * 2, h], v[ch * 2 + 1, h], 64)
            for y1 in range(2):
                s0, s1 = swapped(p[y1, 0], p[y1, 1], 16)
                y00, y01 = swapped(s0, s1, 32)
                target[tile * 4 + y1 * 2, :, ch * 128 : ch * 128 + 128] = y00
                target[tile * 4 + y1 * 2 + 1, :, ch * 128 : ch * 128 + 128] = y01
        for y in range(4):
            right = edge_high if y == 0 else pltpu.roll(edge_high, 128 - 32 * y, 1)
            left = pltpu.roll(edge_low, (96 - 32 * y) % 128, 1) if y != 3 else edge_low
            target[tile * 4 + y, :, 256:384] = jnp.where(lane < 64, right, left)

    def gather_both(tile, carry):
        gather(me, own, tile)
        gather(1 - me, other, tile)
        return carry

    lax.fori_loop(0, 18, gather_both, 0)

    def beside(ref, y, weight=None):
        center = ref[y]
        sides = pltpu.roll(center, 1, 1) + pltpu.roll(center, 383, 1)
        total = sides + (ref[y - 1] + ref[y + 1])
        return total if weight is None else total * weight

    def first(y, carry):
        work[0, y] = own[y] * own_c[2] + other[y] * other_c[2] + beside(own, y, own_c[3])
        return carry

    def second(y, carry):
        work[1, y] = own[y] * own_c[1] + other[y] * other_c[1] + beside(work.at[0], y)
        return carry

    def third(y, carry):
        value = own[y] * own_c[0] + other[y] * other_c[0] + beside(work.at[1], y)
        for half in range(2):
            spread[pl.ds(half * 1024 + y - 4, 16, stride=64), :] = value[:, half * 128 : half * 128 + 128]
        return carry

    lax.fori_loop(2, 70, first, 0)
    lax.fori_loop(3, 69, second, 0)
    lax.fori_loop(4, 68, third, 0)
    for half in range(2):
        out[0, :, half * 128 : half * 128 + 128] = spread[pl.ds(half * 1024, 1024), :]


def smooth(field, low, high):
    return pl.pallas_call(
        smooth_kernel,
        out_shape=jax.ShapeDtypeStruct((1, 1024, 256), jnp.float32),
        scratch_shapes=[
            pltpu.VMEM((72, 16, 384), jnp.float32),
            pltpu.VMEM((72, 16, 384), jnp.float32),
            pltpu.VMEM((2, 72, 16, 384), jnp.float32),
            pltpu.VMEM((2048, 128), jnp.float32),
        ],
        compiler_params=pltpu.CompilerParams(vmem_limit_bytes=VMEM_LIMIT),
        name="smooth",
    )(field, low, high)


def ring(value, axis, steps):
    count = lax.axis_size(axis)
    return lax.ppermute(value, axis, [(i, (i + steps) % count) for i in range(count)])


def shards(velocity_hat):
    x_matrix, x_twist, y_matrix, y_twist = (jnp.asarray(t) for t in tables())
    rows_local = velocity_hat.shape[3]
    parts = velocity_hat.reshape(3, 2, rows_local, GRID)
    next_v = ring(parts[1:2], "gz", 1)
    next_u = ring(parts[0:1], "gz", 1)

    def exchanged(array):
        return lax.all_to_all(array, ("row", "col"), split_axis=0, concat_axis=0, tiled=True)

    line_2 = exchanged(x_transform(2, [(parts, 0), (parts, 1)], x_matrix, x_twist))
    line_0 = exchanged(x_transform(0, [(parts, 2), (parts, 1), (next_v, 0)], x_matrix, x_twist))
    line_1 = exchanged(x_transform(1, [(parts, 2), (parts, 0), (next_u, 0)], x_matrix, x_twist))
    magnitude = y_transform([line_2, line_0, line_1], y_matrix, y_twist)
    field = lax.all_to_all(magnitude, ("gz", "col"), split_axis=0, concat_axis=0, tiled=True)
    by_source = field.reshape(2, 4, 32, 2304)
    high = ring(by_source[:, 0, 0:16], "row", -1)
    low = ring(by_source[:, 3, 16:32], "row", 1)
    return smooth(field, low, high)


def solution(mesh):
    return jax.shard_map(
        shards,
        mesh=mesh,
        in_specs=(P(None, None, "gz", ("row", "col"), None),),
        out_specs=P("gz", "col", "row"),
        check_vma=False,
    )
```

```python
import math

import jax
import jax.numpy as jnp
import numpy as np
from jax import lax
from jax.experimental import pallas as pl
from jax.experimental.pallas import tpu as pltpu
from jax.sharding import PartitionSpec as P

GRID = 4096
RELAX = 0.15
VMEM_LIMIT = 48 * 1024 * 1024
NT = (((1,), (1,)), ((), ()))


def split_bf16(table):
    high = table.astype(jnp.bfloat16)
    low = (table - high.astype(np.float64)).astype(jnp.bfloat16)
    return np.concatenate([high, low], axis=0)


def tables():
    k = np.arange(128)
    blocks = []
    for s in range(2):
        angle = 2 * np.pi * ((np.arange(64)[:, None] * 2 + s) * k[None, :] % 128) / 128
        c, d = np.cos(angle), np.sin(angle)
        blocks.append(np.concatenate([c, -d], axis=1))
        blocks.append(np.concatenate([d, c], axis=1))
    x_matrix = split_bf16(np.concatenate(blocks, axis=0))
    angle = 2 * np.pi * (np.arange(32)[:, None] * k[None, :]) / 4096
    x_twist = np.stack([np.cos(angle), np.sin(angle)]).astype(np.float32) / 64
    j = np.arange(64)
    angle = 2 * np.pi * (j[:, None] * j[None, :] % 64) / 64
    zero = np.zeros((64, 64))
    c, d = np.cos(angle), -np.sin(angle)
    y_matrix = split_bf16(
        np.concatenate(
            [np.concatenate([c, zero, d, zero], axis=1), np.concatenate([zero, c, zero, d], axis=1)], axis=0
        )
    )
    angle = 2 * np.pi * (j[:, None] * j[None, :]) / 4096
    y_twist = np.stack([np.cos(angle), np.sin(angle)]).astype(np.float32) / 64
    y_twist = np.concatenate([y_twist, y_twist], axis=2)
    return x_matrix, x_twist, y_matrix, y_twist


def turned(value, num, den):
    re, im = value
    num = num % den
    if num == 0:
        return value
    if 2 * num == den:
        return (-re, -im)
    if 4 * num == den:
        return (-im, re)
    if 4 * num == 3 * den:
        return (im, -re)
    if 8 * num == den:
        r = math.sqrt(0.5)
        return ((re - im) * r, (re + im) * r)
    if 8 * num == 3 * den:
        r = math.sqrt(0.5)
        return ((re + im) * -r, (re - im) * r)
    c, s = math.cos(2 * math.pi * num / den), math.sin(2 * math.pi * num / den)
    return (re * c - im * s, re * s + im * c)


def plus(a, b):
    return (a[0] + b[0], a[1] + b[1])


def minus(a, b):
    return (a[0] - b[0], a[1] - b[1])


def dft4(v):
    a, b = plus(v[0], v[2]), minus(v[0], v[2])
    c, d = plus(v[1], v[3]), minus(v[1], v[3])
    return [plus(a, c), (b[0] - d[1], b[1] + d[0]), minus(a, c), (b[0] + d[1], b[1] - d[0])]


def dft8(v):
    even, odd = dft4(v[0::2]), dft4(v[1::2])
    odd = [turned(odd[t], t, 8) for t in range(4)]
    return [plus(e, o) for e, o in zip(even, odd)] + [minus(e, o) for e, o in zip(even, odd)]


def x_kernel(which, rows_local, *refs):
    n_in = 2 if which == 2 else 3
    ins, (matrix, twist, out, stage, lines, spread) = refs[:n_in], refs[n_in:]
    step = pl.program_id(0)
    scale = 2.0 * math.pi / GRID
    lane = lax.broadcasted_iota(jnp.int32, (16, 128), 1)
    row = lax.broadcasted_iota(jnp.int32, (16, 128), 0)
    start = lax.axis_index(("row", "col")) * rows_local + step * 16
    ky = row + start
    wave_y = jnp.where(ky >= GRID // 2, ky - GRID, ky).astype(jnp.float32) * scale

    def tile(ref, part, q):
        return ref[0, part, :, pl.ds(q * 128, 128)].astype(jnp.float32)

    def wave_x(q):
        base = q * 128 - (GRID if q >= 16 else 0)
        return (lane + base).astype(jnp.float32) * scale

    def curl(q):
        if which == 2:
            u, v = ins
            wx = wave_x(q)
            return (
                wave_y * tile(u, 1, q) - wx * tile(v, 1, q),
                wx * tile(v, 0, q) - wave_y * tile(u, 0, q),
            )
        w, f, g = ins
        step_re = tile(g, 0, q) - tile(f, 0, q)
        step_im = tile(g, 1, q) - tile(f, 1, q)
        if which == 0:
            return (-wave_y * tile(w, 1, q) - step_re, wave_y * tile(w, 0, q) - step_im)
        wx = wave_x(q)
        return (step_re + wx * tile(w, 1, q), step_im - wx * tile(w, 0, q))

    for a in range(8):
        for b, value in enumerate(dft4([curl(a + 8 * t) for t in range(4)])):
            value = turned(value, a * b, 32)
            stage[0, b * 8 + a] = value[0]
            stage[1, b * 8 + a] = value[1]
    for b in range(4):
        for t, value in enumerate(dft8([(stage[0, b * 8 + a], stage[1, b * 8 + a]) for a in range(8)])):
            n = b + 4 * t
            c, s = twist[0, n : n + 1, :], twist[1, n : n + 1, :]
            at = pl.ds(((n % 16) * 2 + n // 16) * 64 + step * 16, 16)
            lines[at, 0:128] = (value[0] * c - value[1] * s).astype(jnp.bfloat16)
            lines[at, 128:256] = (value[0] * s + value[1] * c).astype(jnp.bfloat16)

    @pl.when(step == 3)
    def _():
        for pair in range(8):
            got = lax.dot_general(
                matrix[...], lines[pl.ds(pair * 256, 256), :], NT, preferred_element_type=jnp.float32
            )
            got = got[0:256] + got[256:512]
            for half in range(2):
                n16 = pair * 2 + half
                for s in range(2):
                    for c in range(2):
                        at = (s * 2 + c) * 64
                        spread[pl.ds(c * 32 + s * 16 + n16, 64, stride=64), :] = got[
                            at : at + 64, half * 128 : half * 128 + 128
                        ]
        for b in range(64):
            out[b] = spread[pl.ds(b * 64, 64), :].astype(jnp.bfloat16)


def x_transform(which, fields, x_matrix, x_twist):
    rows_local = fields[0][0].shape[2]
    specs = [
        pl.BlockSpec((1, 2, 16, GRID), lambda i, comp=comp: (comp, 0, i, 0)) for _, comp in fields
    ] + [
        pl.BlockSpec((512, 256), lambda i: (0, 0)),
        pl.BlockSpec((2, 32, 128), lambda i: (0, 0, 0)),
    ]
    return pl.pallas_call(
        lambda *refs: x_kernel(which, rows_local, *refs),
        grid=(rows_local // 16,),
        in_specs=specs,
        out_specs=pl.BlockSpec((64, 64, 128), lambda i: (0, 0, 0)),
        out_shape=jax.ShapeDtypeStruct((64, 64, 128), jnp.bfloat16),
        scratch_shapes=[
            pltpu.VMEM((2, 32, 16, 128), jnp.float32),
            pltpu.VMEM((2048, 256), jnp.bfloat16),
            pltpu.VMEM((4096, 128), jnp.float32),
        ],
        compiler_params=pltpu.CompilerParams(vmem_limit_bytes=VMEM_LIMIT),
        name=f"curl_x_{which}",
    )(*[array for array, _ in fields], x_matrix, x_twist)


def y_lines(source, twist, stage, lines):
    def one(part, carry):
        def load(c, d):
            return source[d, pl.ds(c * 32 + part * 16, 16), :].astype(jnp.float32)

        for a in range(8):
            values = [(load(0, a + 8 * t), load(1, a + 8 * t)) for t in range(8)]
            for b, value in enumerate(dft8(values)):
                value = turned(value, a * b, 64)
                stage[0, b * 8 + a] = value[0]
                stage[1, b * 8 + a] = value[1]
        for b in range(8):
            for t, value in enumerate(dft8([(stage[0, b * 8 + a], stage[1, b * 8 + a]) for a in range(8)])):
                n = b + 8 * t
                c, s = twist[0, n : n + 1, :], twist[1, n : n + 1, :]
                at = pl.ds(n * 32 + part * 16, 16)
                lines[at, 0:128] = (value[0] * c - value[1] * s).astype(jnp.bfloat16)
                lines[at, 128:256] = (value[0] * s + value[1] * c).astype(jnp.bfloat16)
        return carry

    lax.fori_loop(0, 2, one, 0)


def y_squares(source, matrix, twist, stage, lines, add):
    y_lines(source, twist, stage, lines)
    for chunk in range(8):
        got = lax.dot_general(
            matrix[...], lines[pl.ds(chunk * 256, 256), :], NT, preferred_element_type=jnp.float32
        )
        got = got[0:128] + got[128:256]
        add((slice(None), slice(chunk * 256, chunk * 256 + 256)), got * got)


def y_first(source, matrix, twist, out, stage, lines):
    def add(at, square):
        out[at] = 1.0 + square

    y_squares(source, matrix, twist, stage, lines, add)


def y_next(source, before, matrix, twist, out, stage, lines):
    def add(at, square):
        out[at] = before[at] + square

    y_squares(source, matrix, twist, stage, lines, add)


def y_last(source, before, matrix, twist, out, stage, lines, total):
    def add(at, square):
        total[at] = jnp.sqrt(before[at] + square)

    y_squares(source, matrix, twist, stage, lines, add)

    def put(h, tile, value):
        value = value.astype(jnp.bfloat16)
        for c in range(4):
            for z in range(2):
                out[z * 4 + c, h * 16 : h * 16 + 16, tile * 128 : tile * 128 + 128] = value[c * 16 : c * 16 + 16]

    for h in range(2):
        rows = slice(h * 64, h * 64 + 64)
        for tile in range(16):
            put(h, tile + 1, total[rows, tile * 128 : tile * 128 + 128])
        put(h, 0, pltpu.roll(total[rows, 15 * 128 : 16 * 128], 1, 0))
        put(h, 17, pltpu.roll(total[rows, 0:128], 63, 0))


def y_transform(kernel, source, before, y_matrix, y_twist):
    last = kernel is y_last
    sums = jax.ShapeDtypeStruct((128, 2048), jnp.float32)
    scratch = [pltpu.VMEM((2, 64, 16, 128), jnp.float32), pltpu.VMEM((2048, 256), jnp.bfloat16)]
    return pl.pallas_call(
        kernel,
        out_shape=jax.ShapeDtypeStruct((8, 32, 2304), jnp.bfloat16) if last else sums,
        scratch_shapes=scratch + ([pltpu.VMEM((128, 2048), jnp.float32)] if last else []),
        compiler_params=pltpu.CompilerParams(vmem_limit_bytes=VMEM_LIMIT),
        cost_estimate=pl.CostEstimate(flops=2**28, bytes_accessed=2**22, transcendentals=0),
        name=kernel.__name__,
    )(source, *before, y_matrix, y_twist)


def smooth_coefficients():
    w = RELAX
    even = np.polynomial.polynomial.polypow([1 - 6 * w + 2 * w, w], 3)
    odd = np.polynomial.polynomial.polypow([1 - 6 * w - 2 * w, w], 3)
    return (even + odd) / 2, (even - odd) / 2


def regroup_kernel(field, own, other):
    me = lax.axis_index("gz")
    lane = lax.broadcasted_iota(jnp.int32, (16, 128), 1)

    def swapped(a, b, width):
        upper = (lane & width) != 0
        return (
            jnp.where(upper, pltpu.roll(b, width, 1), a),
            jnp.where(upper, b, pltpu.roll(a, 128 - width, 1)),
        )

    def regroup(z, target, tile):
        at = pl.ds(pl.multiple_of(tile * 128, 128), 128)
        for ch in range(2):
            v = {
                (c, h): field[z * 4 + ch * 2 + c, h * 16 : h * 16 + 16, at].astype(jnp.float32)
                for c in range(2)
                for h in range(2)
            }
            p = {}
            for h in range(2):
                p[0, h], p[1, h] = swapped(v[0, h], v[1, h], 64)
            for y1 in range(2):
                s0, s1 = swapped(p[y1, 0], p[y1, 1], 16)
                y00, y01 = swapped(s0, s1, 32)
                target[tile * 4 + y1 * 2, :, ch * 128 : ch * 128 + 128] = y00
                target[tile * 4 + y1 * 2 + 1, :, ch * 128 : ch * 128 + 128] = y01

    def both(step, carry):
        for t in range(3):
            regroup(me, own, step * 3 + t)
            regroup(1 - me, other, step * 3 + t)
        return carry

    lax.fori_loop(0, 6, both, 0)


def regroup(field):
    return pl.pallas_call(
        regroup_kernel,
        out_shape=[jax.ShapeDtypeStruct((72, 16, 256), jnp.float32)] * 2,
        compiler_params=pltpu.CompilerParams(vmem_limit_bytes=VMEM_LIMIT),
        cost_estimate=pl.CostEstimate(flops=2**24, bytes_accessed=2**23, transcendentals=0),
        name="regroup",
    )(field)


def smooth_kernel(own, other, low, high, out, own_edge, other_edge, work, spread):
    own_c, other_c = [[float(v) for v in part] for part in smooth_coefficients()]
    me = lax.axis_index("gz")
    lane = lax.broadcasted_iota(jnp.int32, (16, 128), 1)

    def edges(step, carry):
        for t in range(3):
            tile = step * 3 + t
            at = pl.ds(pl.multiple_of(tile * 128, 128), 128)
            for z, target in ((me, own_edge), (1 - me, other_edge)):
                left = low[z, :, at].astype(jnp.float32)
                right = high[z, :, at].astype(jnp.float32)
                for y in range(4):
                    target[tile * 4 + y] = jnp.where(
                        lane < 64,
                        pltpu.roll(right, 128 - 32 * y, 1) if y else right,
                        pltpu.roll(left, 96 - 32 * y, 1) if y < 3 else left,
                    )
        return carry

    lax.fori_loop(0, 6, edges, 0)

    def beside(ref, y, center):
        sides = pltpu.roll(center, 1, 1) + pltpu.roll(center, 383, 1)
        return sides + (ref(y - 1) + ref(y + 1))

    def own_at(y):
        return jnp.concatenate([own[y], own_edge[y]], axis=1)

    def other_at(y):
        return jnp.concatenate([other[y], other_edge[y]], axis=1)

    def each(begin, end, unroll, body):
        def some(step, carry):
            for t in range(unroll):
                body(begin + step * unroll + t)
            return carry

        lax.fori_loop(0, (end - begin) // unroll, some, 0)

    def first(y):
        center = own_at(y)
        work[0, y] = center * own_c[2] + other_at(y) * other_c[2] + beside(own_at, y, center) * own_c[3]

    def second(y):
        center = work[0, y]
        work[1, y] = own_at(y) * own_c[1] + other_at(y) * other_c[1] + beside(lambda i: work[0, i], y, center)

    def third(y):
        center = work[1, y]
        value = beside(lambda i: work[1, i], y, center)[:, 0:256]
        value = own[y] * own_c[0] + other[y] * other_c[0] + value
        for half in range(2):
            spread[pl.ds(half * 1024 + y - 4, 16, stride=64), :] = value[:, half * 128 : half * 128 + 128]

    each(2, 70, 4, first)
    each(3, 69, 6, second)
    each(4, 68, 4, third)
    for half in range(2):
        out[0, :, half * 128 : half * 128 + 128] = spread[pl.ds(half * 1024, 1024), :]


def smooth(own, other, low, high):
    return pl.pallas_call(
        smooth_kernel,
        out_shape=jax.ShapeDtypeStruct((1, 1024, 256), jnp.float32),
        scratch_shapes=[
            pltpu.VMEM((72, 16, 128), jnp.float32),
            pltpu.VMEM((72, 16, 128), jnp.float32),
            pltpu.VMEM((2, 72, 16, 384), jnp.float32),
            pltpu.VMEM((2048, 128), jnp.float32),
        ],
        compiler_params=pltpu.CompilerParams(vmem_limit_bytes=VMEM_LIMIT),
        name="smooth",
    )(own, other, low, high)


def copy_kernel(parts, u, v, sems):
    copies = [
        pltpu.make_async_copy(parts.at[pl.ds(i, 1)], target, sems.at[i]) for i, target in enumerate((u, v))
    ]
    for copy in copies:
        copy.start()
    for copy in copies:
        copy.wait()


def copy_uv(parts):
    shape = jax.ShapeDtypeStruct((1,) + parts.shape[1:], parts.dtype)
    return pl.pallas_call(
        copy_kernel,
        in_specs=[pl.BlockSpec(memory_space=pl.ANY)],
        out_specs=[pl.BlockSpec(memory_space=pltpu.VMEM)] * 2,
        out_shape=[shape, shape],
        scratch_shapes=[pltpu.SemaphoreType.DMA((2,))],
        compiler_params=pltpu.CompilerParams(vmem_limit_bytes=VMEM_LIMIT),
        name="copy_uv",
    )(parts)


def ring(value, axis, steps):
    count = lax.axis_size(axis)
    return lax.ppermute(value, axis, [(i, (i + steps) % count) for i in range(count)])


def shards(velocity_hat):
    x_matrix, x_twist, y_matrix, y_twist = (jnp.asarray(t) for t in tables())
    rows_local = velocity_hat.shape[3]
    parts = velocity_hat.reshape(3, 2, rows_local, GRID)
    u, v = copy_uv(parts)
    next_u = ring(u, "gz", 1)
    next_v = ring(v, "gz", 1)

    def exchanged(array):
        return lax.all_to_all(array, ("row", "col"), split_axis=0, concat_axis=0, tiled=True)

    line_2 = exchanged(x_transform(2, [(parts, 0), (parts, 1)], x_matrix, x_twist))
    line_1 = exchanged(x_transform(1, [(parts, 2), (parts, 0), (next_u, 0)], x_matrix, x_twist))
    line_0 = exchanged(x_transform(0, [(parts, 2), (parts, 1), (next_v, 0)], x_matrix, x_twist))
    squares = y_transform(y_first, line_2, (), y_matrix, y_twist)
    squares = y_transform(y_next, line_1, (squares,), y_matrix, y_twist)
    magnitude = y_transform(y_last, line_0, (squares,), y_matrix, y_twist)
    field = lax.all_to_all(magnitude, ("gz", "col"), split_axis=0, concat_axis=0, tiled=True)
    by_source = field.reshape(2, 4, 32, 2304)
    high = ring(by_source[:, 0, 0:16], "row", -1)
    low = ring(by_source[:, 3, 16:32], "row", 1)
    own, other = regroup(field)
    return smooth(own, other, low, high)


def solution(mesh):
    return jax.shard_map(
        shards,
        mesh=mesh,
        in_specs=(P(None, None, "gz", ("row", "col"), None),),
        out_specs=P("gz", "col", "row"),
        check_vma=False,
    )
```

```python
import math

import jax
import jax.numpy as jnp
import numpy as np
from jax import lax
from jax.experimental import pallas as pl
from jax.experimental.pallas import tpu as pltpu
from jax.sharding import PartitionSpec as P

GRID = 4096
RELAX = 0.15
VMEM_LIMIT = 48 * 1024 * 1024
NT = (((1,), (1,)), ((), ()))


def split_bf16(table):
    high = table.astype(jnp.bfloat16)
    low = (table - high.astype(np.float64)).astype(jnp.bfloat16)
    return np.concatenate([high, low], axis=0)


def tables():
    k = np.arange(128)
    blocks = []
    for s in range(2):
        angle = 2 * np.pi * ((np.arange(64)[:, None] * 2 + s) * k[None, :] % 128) / 128
        c, d = np.cos(angle), np.sin(angle)
        blocks.append(np.concatenate([c, -d], axis=1))
        blocks.append(np.concatenate([d, c], axis=1))
    x_matrix = split_bf16(np.concatenate(blocks, axis=0))
    angle = 2 * np.pi * (np.arange(32)[:, None] * k[None, :]) / 4096
    x_twist = np.stack([np.cos(angle), np.sin(angle)]).astype(np.float32) / 64
    j = np.arange(64)
    angle = 2 * np.pi * (j[:, None] * j[None, :] % 64) / 64
    zero = np.zeros((64, 64))
    c, d = np.cos(angle), -np.sin(angle)
    y_matrix = split_bf16(
        np.concatenate(
            [np.concatenate([c, zero, d, zero], axis=1), np.concatenate([zero, c, zero, d], axis=1)], axis=0
        )
    )
    angle = 2 * np.pi * (j[:, None] * j[None, :]) / 4096
    y_twist = np.stack([np.cos(angle), np.sin(angle)]).astype(np.float32) / 64
    y_twist = np.concatenate([y_twist, y_twist], axis=2)
    return x_matrix, x_twist, y_matrix, y_twist


def turned(value, num, den):
    re, im = value
    num = num % den
    if num == 0:
        return value
    if 2 * num == den:
        return (-re, -im)
    if 4 * num == den:
        return (-im, re)
    if 4 * num == 3 * den:
        return (im, -re)
    if 8 * num == den:
        r = math.sqrt(0.5)
        return ((re - im) * r, (re + im) * r)
    if 8 * num == 3 * den:
        r = math.sqrt(0.5)
        return ((re + im) * -r, (re - im) * r)
    c, s = math.cos(2 * math.pi * num / den), math.sin(2 * math.pi * num / den)
    return (re * c - im * s, re * s + im * c)


def plus(a, b):
    return (a[0] + b[0], a[1] + b[1])


def minus(a, b):
    return (a[0] - b[0], a[1] - b[1])


def dft4(v):
    a, b = plus(v[0], v[2]), minus(v[0], v[2])
    c, d = plus(v[1], v[3]), minus(v[1], v[3])
    return [plus(a, c), (b[0] - d[1], b[1] + d[0]), minus(a, c), (b[0] + d[1], b[1] - d[0])]


def dft8(v):
    even, odd = dft4(v[0::2]), dft4(v[1::2])
    odd = [turned(odd[t], t, 8) for t in range(4)]
    return [plus(e, o) for e, o in zip(even, odd)] + [minus(e, o) for e, o in zip(even, odd)]


def x_kernel(which, rows_local, *refs):
    n_in = 2 if which == 2 else 3
    ins, (matrix, twist, out, stage, lines, spread, packed, sems) = refs[:n_in], refs[n_in:]
    step = pl.program_id(0)
    scale = 2.0 * math.pi / GRID
    lane = lax.broadcasted_iota(jnp.int32, (16, 128), 1)
    row = lax.broadcasted_iota(jnp.int32, (16, 128), 0)
    start = lax.axis_index(("row", "col")) * rows_local + step * 16
    ky = row + start
    wave_y = jnp.where(ky >= GRID // 2, ky - GRID, ky).astype(jnp.float32) * scale

    def tile(ref, part, q):
        return ref[0, part, :, pl.ds(q * 128, 128)].astype(jnp.float32)

    def wave_x(q):
        base = q * 128 - (GRID if q >= 16 else 0)
        return (lane + base).astype(jnp.float32) * scale

    def curl(q):
        if which == 2:
            u, v = ins
            wx = wave_x(q)
            return (
                wave_y * tile(u, 1, q) - wx * tile(v, 1, q),
                wx * tile(v, 0, q) - wave_y * tile(u, 0, q),
            )
        w, f, g = ins
        step_re = tile(g, 0, q) - tile(f, 0, q)
        step_im = tile(g, 1, q) - tile(f, 1, q)
        if which == 0:
            return (-wave_y * tile(w, 1, q) - step_re, wave_y * tile(w, 0, q) - step_im)
        wx = wave_x(q)
        return (step_re + wx * tile(w, 1, q), step_im - wx * tile(w, 0, q))

    for a in range(8):
        for b, value in enumerate(dft4([curl(a + 8 * t) for t in range(4)])):
            value = turned(value, a * b, 32)
            stage[0, b * 8 + a] = value[0]
            stage[1, b * 8 + a] = value[1]
    for b in range(4):
        for t, value in enumerate(dft8([(stage[0, b * 8 + a], stage[1, b * 8 + a]) for a in range(8)])):
            n = b + 4 * t
            c, s = twist[0, n : n + 1, :], twist[1, n : n + 1, :]
            at = pl.ds(((n % 16) * 2 + n // 16) * 64 + step * 16, 16)
            lines[at, 0:128] = (value[0] * c - value[1] * s).astype(jnp.bfloat16)
            lines[at, 128:256] = (value[0] * s + value[1] * c).astype(jnp.bfloat16)

    @pl.when(step == 3)
    def _():
        for pair in range(8):
            got = lax.dot_general(
                matrix[...], lines[pl.ds(pair * 256, 256), :], NT, preferred_element_type=jnp.float32
            )
            got = got[0:256] + got[256:512]
            for half in range(2):
                n16 = pair * 2 + half
                for s in range(2):
                    for c in range(2):
                        at = (s * 2 + c) * 64
                        spread[pl.ds(c * 32 + s * 16 + n16, 64, stride=64), :] = got[
                            at : at + 64, half * 128 : half * 128 + 128
                        ]
        copies = []
        for group in range(4):
            for b in range(group * 16, group * 16 + 16):
                packed[b] = spread[pl.ds(b * 64, 64), :].astype(jnp.bfloat16)
            at = pl.ds(group * 16, 16)
            copies.append(pltpu.make_async_copy(packed.at[at], out.at[at], sems.at[group]))
            copies[-1].start()
        for copy in copies:
            copy.wait()


def x_transform(which, fields, x_matrix, x_twist):
    rows_local = fields[0][0].shape[2]
    specs = [
        pl.BlockSpec((1, 2, 16, GRID), lambda i, comp=comp: (comp, 0, i, 0)) for _, comp in fields
    ] + [
        pl.BlockSpec((512, 256), lambda i: (0, 0)),
        pl.BlockSpec((2, 32, 128), lambda i: (0, 0, 0)),
    ]
    return pl.pallas_call(
        lambda *refs: x_kernel(which, rows_local, *refs),
        grid=(rows_local // 16,),
        in_specs=specs,
        out_specs=pl.BlockSpec(memory_space=pltpu.HBM),
        out_shape=jax.ShapeDtypeStruct((64, 64, 128), jnp.bfloat16),
        scratch_shapes=[
            pltpu.VMEM((2, 32, 16, 128), jnp.float32),
            pltpu.VMEM((2048, 256), jnp.bfloat16),
            pltpu.VMEM((4096, 128), jnp.float32),
            pltpu.VMEM((64, 64, 128), jnp.bfloat16),
            pltpu.SemaphoreType.DMA((4,)),
        ],
        compiler_params=pltpu.CompilerParams(vmem_limit_bytes=VMEM_LIMIT),
        name=f"curl_x_{which}",
    )(*[array for array, _ in fields], x_matrix, x_twist)


def y_lines(source, twist, stage, lines):
    def one(part, carry):
        def load(c, d):
            return source[d, pl.ds(c * 32 + part * 16, 16), :].astype(jnp.float32)

        for a in range(8):
            values = [(load(0, a + 8 * t), load(1, a + 8 * t)) for t in range(8)]
            for b, value in enumerate(dft8(values)):
                value = turned(value, a * b, 64)
                stage[0, b * 8 + a] = value[0]
                stage[1, b * 8 + a] = value[1]
        for b in range(8):
            for t, value in enumerate(dft8([(stage[0, b * 8 + a], stage[1, b * 8 + a]) for a in range(8)])):
                n = b + 8 * t
                c, s = twist[0, n : n + 1, :], twist[1, n : n + 1, :]
                at = pl.ds(n * 32 + part * 16, 16)
                lines[at, 0:128] = (value[0] * c - value[1] * s).astype(jnp.bfloat16)
                lines[at, 128:256] = (value[0] * s + value[1] * c).astype(jnp.bfloat16)
        return carry

    lax.fori_loop(0, 2, one, 0)


def y_squares(source, matrix, twist, stage, lines, add):
    y_lines(source, twist, stage, lines)
    for chunk in range(8):
        got = lax.dot_general(
            matrix[...], lines[pl.ds(chunk * 256, 256), :], NT, preferred_element_type=jnp.float32
        )
        got = got[0:128] + got[128:256]
        add((slice(None), slice(chunk * 256, chunk * 256 + 256)), got * got)


def y_first(source, matrix, twist, out, stage, lines):
    def add(at, square):
        out[at] = 1.0 + square

    y_squares(source, matrix, twist, stage, lines, add)


def y_next(source, before, matrix, twist, out, stage, lines):
    def add(at, square):
        out[at] = before[at] + square

    y_squares(source, matrix, twist, stage, lines, add)


def y_last(source, before, matrix, twist, out, stage, lines, total):
    def add(at, square):
        total[at] = jnp.sqrt(before[at] + square)

    y_squares(source, matrix, twist, stage, lines, add)

    def put(h, tile, value):
        value = value.astype(jnp.bfloat16)
        for c in range(4):
            for z in range(2):
                out[z * 4 + c, h * 16 : h * 16 + 16, tile * 128 : tile * 128 + 128] = value[c * 16 : c * 16 + 16]

    for h in range(2):
        rows = slice(h * 64, h * 64 + 64)
        for tile in range(16):
            put(h, tile + 1, total[rows, tile * 128 : tile * 128 + 128])
        put(h, 0, pltpu.roll(total[rows, 15 * 128 : 16 * 128], 1, 0))
        put(h, 17, pltpu.roll(total[rows, 0:128], 63, 0))


def y_transform(kernel, source, before, y_matrix, y_twist):
    last = kernel is y_last
    sums = jax.ShapeDtypeStruct((128, 2048), jnp.float32)
    scratch = [pltpu.VMEM((2, 64, 16, 128), jnp.float32), pltpu.VMEM((2048, 256), jnp.bfloat16)]
    return pl.pallas_call(
        kernel,
        out_shape=jax.ShapeDtypeStruct((8, 32, 2304), jnp.bfloat16) if last else sums,
        scratch_shapes=scratch + ([pltpu.VMEM((128, 2048), jnp.float32)] if last else []),
        compiler_params=pltpu.CompilerParams(vmem_limit_bytes=VMEM_LIMIT),
        cost_estimate=pl.CostEstimate(flops=2**28, bytes_accessed=2**22, transcendentals=0),
        name=kernel.__name__,
    )(source, *before, y_matrix, y_twist)


def smooth_coefficients():
    w = RELAX
    even = np.polynomial.polynomial.polypow([1 - 6 * w + 2 * w, w], 3)
    odd = np.polynomial.polynomial.polypow([1 - 6 * w - 2 * w, w], 3)
    return (even + odd) / 2, (even - odd) / 2


def regroup_kernel(field, own, other):
    me = lax.axis_index("gz")
    lane = lax.broadcasted_iota(jnp.int32, (16, 128), 1)

    def swapped(a, b, width):
        upper = (lane & width) != 0
        return (
            jnp.where(upper, pltpu.roll(b, width, 1), a),
            jnp.where(upper, b, pltpu.roll(a, 128 - width, 1)),
        )

    def regroup(z, target, tile):
        at = pl.ds(pl.multiple_of(tile * 128, 128), 128)
        for ch in range(2):
            v = {
                (c, h): field[z * 4 + ch * 2 + c, h * 16 : h * 16 + 16, at].astype(jnp.float32)
                for c in range(2)
                for h in range(2)
            }
            p = {}
            for h in range(2):
                p[0, h], p[1, h] = swapped(v[0, h], v[1, h], 64)
            for y1 in range(2):
                s0, s1 = swapped(p[y1, 0], p[y1, 1], 16)
                y00, y01 = swapped(s0, s1, 32)
                target[tile * 4 + y1 * 2, :, ch * 128 : ch * 128 + 128] = y00
                target[tile * 4 + y1 * 2 + 1, :, ch * 128 : ch * 128 + 128] = y01

    def both(step, carry):
        for t in range(3):
            regroup(me, own, step * 3 + t)
            regroup(1 - me, other, step * 3 + t)
        return carry

    lax.fori_loop(0, 6, both, 0)


def regroup(field):
    return pl.pallas_call(
        regroup_kernel,
        out_shape=[jax.ShapeDtypeStruct((72, 16, 256), jnp.float32)] * 2,
        compiler_params=pltpu.CompilerParams(vmem_limit_bytes=VMEM_LIMIT),
        cost_estimate=pl.CostEstimate(flops=2**24, bytes_accessed=2**23, transcendentals=0),
        name="regroup",
    )(field)


def edge_kernel(field, low, high):
    lane = lax.broadcasted_iota(jnp.int32, (16, 128), 1)
    for z in range(2):
        for group in range(5):
            last = first = jnp.zeros((16, 128), jnp.float32)
            for t in range(min(4, 18 - group * 4)):
                at = slice((group * 4 + t) * 128, (group * 4 + t) * 128 + 128)
                here = (lane & 24) == 8 * t
                last = jnp.where(here, pltpu.roll(field[z * 4 + 3, 16:32, at].astype(jnp.float32), 100 + 8 * t, 1), last)
                first = jnp.where(here, pltpu.roll(field[z * 4, 0:16, at].astype(jnp.float32), 4 + 8 * t, 1), first)
            low[z, :, group * 128 : group * 128 + 128] = last.astype(jnp.bfloat16)
            high[z, :, group * 128 : group * 128 + 128] = first.astype(jnp.bfloat16)


def edges(field):
    return pl.pallas_call(
        edge_kernel,
        out_shape=[jax.ShapeDtypeStruct((2, 16, 640), jnp.bfloat16)] * 2,
        compiler_params=pltpu.CompilerParams(vmem_limit_bytes=VMEM_LIMIT),
        name="edges",
    )(field)


def smooth_kernel(own, other, low, high, out, own_edge, other_edge, work, spread):
    own_c, other_c = [[float(v) for v in part] for part in smooth_coefficients()]
    me = lax.axis_index("gz")
    lane = lax.broadcasted_iota(jnp.int32, (16, 128), 1)
    is_low = (lane & 7) < 4

    def spread_edges(group, tiles):
        at = pl.ds(pl.multiple_of(group * 128, 128), 128)
        for z, target in ((me, own_edge), (1 - me, other_edge)):
            both = jnp.where(is_low, low[z, :, at].astype(jnp.float32), high[z, :, at].astype(jnp.float32))
            for t in range(tiles):
                for y in range(4):
                    target[(group * 4 + t) * 4 + y] = pltpu.roll(both, 124 - 32 * y - 8 * t, 1)

    def edge_group(group, carry):
        spread_edges(group, 4)
        return carry

    lax.fori_loop(0, 4, edge_group, 0)
    spread_edges(4, 2)

    def beside(ref, y, center):
        sides = pltpu.roll(center, 1, 1) + pltpu.roll(center, 383, 1)
        return sides + (ref(y - 1) + ref(y + 1))

    def own_at(y):
        return jnp.concatenate([own[y], own_edge[y]], axis=1)

    def other_at(y):
        return jnp.concatenate([other[y], other_edge[y]], axis=1)

    def each(begin, end, unroll, body):
        def some(step, carry):
            for t in range(unroll):
                body(begin + step * unroll + t)
            return carry

        lax.fori_loop(0, (end - begin) // unroll, some, 0)

    def first(y):
        center = own_at(y)
        work[0, y] = center * own_c[2] + other_at(y) * other_c[2] + beside(own_at, y, center) * own_c[3]

    def second(y):
        center = work[0, y]
        work[1, y] = own_at(y) * own_c[1] + other_at(y) * other_c[1] + beside(lambda i: work[0, i], y, center)

    def third(y):
        center = work[1, y]
        value = beside(lambda i: work[1, i], y, center)[:, 0:256]
        value = own[y] * own_c[0] + other[y] * other_c[0] + value
        for half in range(2):
            spread[pl.ds(half * 1024 + y - 4, 16, stride=64), :] = value[:, half * 128 : half * 128 + 128]

    each(2, 70, 4, first)
    each(3, 69, 6, second)
    each(4, 68, 4, third)
    for half in range(2):
        out[0, :, half * 128 : half * 128 + 128] = spread[pl.ds(half * 1024, 1024), :]


def smooth(own, other, low, high):
    return pl.pallas_call(
        smooth_kernel,
        out_shape=jax.ShapeDtypeStruct((1, 1024, 256), jnp.float32),
        scratch_shapes=[
            pltpu.VMEM((72, 16, 128), jnp.float32),
            pltpu.VMEM((72, 16, 128), jnp.float32),
            pltpu.VMEM((2, 72, 16, 384), jnp.float32),
            pltpu.VMEM((2048, 128), jnp.float32),
        ],
        compiler_params=pltpu.CompilerParams(vmem_limit_bytes=VMEM_LIMIT),
        name="smooth",
    )(own, other, low, high)


def copy_kernel(parts, uv, sem):
    copy = pltpu.make_async_copy(parts.at[pl.ds(0, 2)], uv, sem)
    copy.start()
    copy.wait()


def copy_uv(parts):
    return pl.pallas_call(
        copy_kernel,
        in_specs=[pl.BlockSpec(memory_space=pltpu.HBM)],
        out_specs=pl.BlockSpec(memory_space=pltpu.VMEM),
        out_shape=jax.ShapeDtypeStruct((2,) + parts.shape[1:], parts.dtype),
        scratch_shapes=[pltpu.SemaphoreType.DMA],
        compiler_params=pltpu.CompilerParams(vmem_limit_bytes=VMEM_LIMIT),
        name="copy_uv",
    )(parts)


def ring(value, axis, steps):
    count = lax.axis_size(axis)
    return lax.ppermute(value, axis, [(i, (i + steps) % count) for i in range(count)])


def shards(velocity_hat):
    x_matrix, x_twist, y_matrix, y_twist = (jnp.asarray(t) for t in tables())
    rows_local = velocity_hat.shape[3]
    parts = velocity_hat.reshape(3, 2, rows_local, GRID)
    uv = copy_uv(parts)
    next_uv = ring(uv, "gz", 1)

    def exchanged(array):
        return lax.all_to_all(array, ("row", "col"), split_axis=0, concat_axis=0, tiled=True)

    line_2 = exchanged(x_transform(2, [(uv, 0), (uv, 1)], x_matrix, x_twist))
    line_1 = exchanged(x_transform(1, [(parts, 2), (uv, 0), (next_uv, 0)], x_matrix, x_twist))
    line_0 = exchanged(x_transform(0, [(parts, 2), (uv, 1), (next_uv, 1)], x_matrix, x_twist))
    squares = y_transform(y_first, line_2, (), y_matrix, y_twist)
    squares = y_transform(y_next, line_1, (squares,), y_matrix, y_twist)
    magnitude = y_transform(y_last, line_0, (squares,), y_matrix, y_twist)
    field = lax.all_to_all(magnitude, ("gz", "col"), split_axis=0, concat_axis=0, tiled=True)
    last, first = edges(field)
    low, high = ring(last, "row", 1), ring(first, "row", -1)
    own, other = regroup(field)
    return smooth(own, other, low, high)


def solution(mesh):
    return jax.shard_map(
        shards,
        mesh=mesh,
        in_specs=(P(None, None, "gz", ("row", "col"), None),),
        out_specs=P("gz", "col", "row"),
        check_vma=False,
    )
```

```python
import math

import jax
import jax.numpy as jnp
import numpy as np
from jax import lax
from jax.experimental import pallas as pl
from jax.experimental.pallas import tpu as pltpu
from jax.sharding import PartitionSpec as P

GRID = 4096
RELAX = 0.15
VMEM_LIMIT = 48 * 1024 * 1024
NT = (((1,), (1,)), ((), ()))


def split_bf16(table):
    high = table.astype(jnp.bfloat16)
    low = (table - high.astype(np.float64)).astype(jnp.bfloat16)
    return np.concatenate([high, low], axis=0)


def tables():
    k = np.arange(128)
    blocks = []
    for s in range(2):
        angle = 2 * np.pi * ((np.arange(64)[:, None] * 2 + s) * k[None, :] % 128) / 128
        c, d = np.cos(angle), np.sin(angle)
        blocks.append(np.concatenate([c, -d], axis=1))
        blocks.append(np.concatenate([d, c], axis=1))
    x_matrix = split_bf16(np.concatenate(blocks, axis=0))
    angle = 2 * np.pi * (np.arange(32)[:, None] * k[None, :]) / 4096
    x_twist = np.stack([np.cos(angle), np.sin(angle)]).astype(np.float32) / 64
    j = np.arange(64)
    angle = 2 * np.pi * (j[:, None] * j[None, :] % 64) / 64
    zero = np.zeros((64, 64))
    c, d = np.cos(angle), -np.sin(angle)
    y_matrix = split_bf16(
        np.concatenate(
            [np.concatenate([c, zero, d, zero], axis=1), np.concatenate([zero, c, zero, d], axis=1)], axis=0
        )
    )
    angle = 2 * np.pi * (j[:, None] * j[None, :]) / 4096
    y_twist = np.stack([np.cos(angle), np.sin(angle)]).astype(np.float32) / 64
    y_twist = np.concatenate([y_twist, y_twist], axis=2)
    return x_matrix, x_twist, y_matrix, y_twist


def turned(value, num, den):
    re, im = value
    num = num % den
    if num == 0:
        return value
    if 2 * num == den:
        return (-re, -im)
    if 4 * num == den:
        return (-im, re)
    if 4 * num == 3 * den:
        return (im, -re)
    if 8 * num == den:
        r = math.sqrt(0.5)
        return ((re - im) * r, (re + im) * r)
    if 8 * num == 3 * den:
        r = math.sqrt(0.5)
        return ((re + im) * -r, (re - im) * r)
    c, s = math.cos(2 * math.pi * num / den), math.sin(2 * math.pi * num / den)
    return (re * c - im * s, re * s + im * c)


def plus(a, b):
    return (a[0] + b[0], a[1] + b[1])


def minus(a, b):
    return (a[0] - b[0], a[1] - b[1])


def dft4(v):
    a, b = plus(v[0], v[2]), minus(v[0], v[2])
    c, d = plus(v[1], v[3]), minus(v[1], v[3])
    return [plus(a, c), (b[0] - d[1], b[1] + d[0]), minus(a, c), (b[0] + d[1], b[1] - d[0])]


def dft8(v):
    even, odd = dft4(v[0::2]), dft4(v[1::2])
    odd = [turned(odd[t], t, 8) for t in range(4)]
    return [plus(e, o) for e, o in zip(even, odd)] + [minus(e, o) for e, o in zip(even, odd)]


def x_kernel(fields, rows_local, *refs):
    n_in = 2 if fields == ("curl_z",) or fields[0] == "u" else 3
    n_out = 2 if len(fields) == 2 else 1
    ins, (matrix, twist), refs = refs[:n_in], refs[n_in : n_in + 2], refs[n_in + 2 :]
    outs, (stage, lines, spread) = refs[-3 - n_out : -3], refs[-3:]
    step = pl.program_id(0)
    scale = 2.0 * math.pi / GRID
    lane = lax.broadcasted_iota(jnp.int32, (16, 128), 1)
    row = lax.broadcasted_iota(jnp.int32, (16, 128), 0)
    start = lax.axis_index(("yh", "zc", "col")) * rows_local + step * 16
    ky = row + start
    wave_y = jnp.where(ky >= GRID // 2, ky - GRID, ky).astype(jnp.float32) * scale

    def tile(ref, part, q):
        return ref[0, part, :, pl.ds(q * 128, 128)].astype(jnp.float32)

    def wave_x(q):
        base = q * 128 - (GRID if q >= 16 else 0)
        return (lane + base).astype(jnp.float32) * scale

    def value_of(field, q):
        if field == "curl_z":
            u, v = ins
            wx = wave_x(q)
            return (
                wave_y * tile(u, 1, q) - wx * tile(v, 1, q),
                wx * tile(v, 0, q) - wave_y * tile(u, 0, q),
            )
        if field == "u":
            return (tile(ins[0], 0, q), tile(ins[0], 1, q))
        if field == "v":
            return (tile(ins[1], 0, q), tile(ins[1], 1, q))
        u, v, w = ins
        if field == "curl_x":
            return (tile(v, 0, q) - wave_y * tile(w, 1, q), tile(v, 1, q) + wave_y * tile(w, 0, q))
        wx = wave_x(q)
        return (wx * tile(w, 1, q) - tile(u, 0, q), -wx * tile(w, 0, q) - tile(u, 1, q))

    for index, field in enumerate(fields):
        for a in range(8):
            for b, value in enumerate(dft4([value_of(field, a + 8 * t) for t in range(4)])):
                value = turned(value, a * b, 32)
                stage[0, b * 8 + a] = value[0]
                stage[1, b * 8 + a] = value[1]
        for b in range(4):
            for t, value in enumerate(dft8([(stage[0, b * 8 + a], stage[1, b * 8 + a]) for a in range(8)])):
                n = b + 4 * t
                c, s = twist[0, n : n + 1, :], twist[1, n : n + 1, :]
                at = pl.ds(((n % 16) * 2 + n // 16) * 64 + step * 16, 16)
                lines[index, at, 0:128] = (value[0] * c - value[1] * s).astype(jnp.bfloat16)
                lines[index, at, 128:256] = (value[0] * s + value[1] * c).astype(jnp.bfloat16)

    @pl.when(step == 3)
    def _():
        for index in range(len(fields)):
            for pair in range(8):
                got = lax.dot_general(
                    matrix[...], lines[index, pl.ds(pair * 256, 256), :], NT, preferred_element_type=jnp.float32
                )
                got = got[0:256] + got[256:512]
                for half in range(2):
                    n16 = pair * 2 + half
                    for s in range(2):
                        for c in range(2):
                            at = (s * 2 + c) * 64
                            spread[pl.ds(c * 32 + s * 16 + n16, 64, stride=64), :] = got[
                                at : at + 64, half * 128 : half * 128 + 128
                            ]
            for half in range(2):
                first = (lax.axis_index("yh") + half) % 2 * 2048
                for b in range(32):
                    at = pl.ds(pl.multiple_of(first + b * 64, 64), 64)
                    block = spread[at, :].astype(jnp.bfloat16)
                    if n_out == 1:
                        outs[0][b, half * 64 : half * 64 + 64, :] = block
                    else:
                        outs[half][b, index * 64 : index * 64 + 64, :] = block


def x_transform(fields, parts, x_matrix, x_twist, after=()):
    rows_local = parts.shape[2]
    comps = (0, 1, 2) if fields[0] == "curl_x" else (0, 1)
    specs = [pl.BlockSpec((1, 2, 16, GRID), lambda i, comp=comp: (comp, 0, i, 0)) for comp in comps] + [
        pl.BlockSpec((512, 256), lambda i: (0, 0)),
        pl.BlockSpec((2, 32, 128), lambda i: (0, 0, 0)),
    ]
    specs += [pl.BlockSpec(memory_space=pl.ANY)] * len(after)
    return pl.pallas_call(
        lambda *refs: x_kernel(fields, rows_local, *refs),
        grid=(rows_local // 16,),
        in_specs=specs,
        out_specs=[pl.BlockSpec((32, 128, 128), lambda i: (0, 0, 0))] * len(fields),
        out_shape=[jax.ShapeDtypeStruct((32, 128, 128), jnp.bfloat16)] * len(fields),
        scratch_shapes=[
            pltpu.VMEM((2, 32, 16, 128), jnp.float32),
            pltpu.VMEM((len(fields), 2048, 256), jnp.bfloat16),
            pltpu.VMEM((4096, 128), jnp.float32),
        ],
        compiler_params=pltpu.CompilerParams(vmem_limit_bytes=VMEM_LIMIT),
        cost_estimate=pl.CostEstimate(flops=2**30, bytes_accessed=2**22, transcendentals=0),
        name="lines_" + "_".join(fields),
    )(*[parts] * len(comps), x_matrix, x_twist, *after)


def meet_kernel(own, came, near, across, out):
    for b in range(out.shape[0]):
        for index, sign in ((0, -1.0), (1, 1.0)):
            rows, term_rows = slice(index * 64, index * 64 + 64), slice(64 - index * 64, 128 - index * 64)
            for half, (field, term) in enumerate(((own, near), (came, across))):
                value = field[b, rows, :].astype(jnp.float32) + sign * term[b, term_rows, :].astype(jnp.float32)
                at = index * 128 + half * 64
                out[b, at : at + 64, :] = value.astype(jnp.bfloat16)


def meet(own, came, near, across):
    return pl.pallas_call(
        meet_kernel,
        grid=(4,),
        in_specs=[pl.BlockSpec((8, 128, 128), lambda i: (i, 0, 0))] * 4,
        out_specs=pl.BlockSpec((8, 256, 128), lambda i: (i, 0, 0)),
        out_shape=jax.ShapeDtypeStruct((32, 256, 128), jnp.bfloat16),
        compiler_params=pltpu.CompilerParams(vmem_limit_bytes=VMEM_LIMIT),
        cost_estimate=pl.CostEstimate(flops=2**20, bytes_accessed=2**22, transcendentals=0),
        name="meet",
    )(own, came, near, across)


def y_lines(sources, twist, stage, lines):
    def one(part, carry):
        def load(c, d):
            source, first = sources[d // 32]
            return source[d % 32, pl.ds(first + c * 32 + part * 16, 16), :].astype(jnp.float32)

        for a in range(8):
            values = [(load(0, a + 8 * t), load(1, a + 8 * t)) for t in range(8)]
            for b, value in enumerate(dft8(values)):
                value = turned(value, a * b, 64)
                stage[0, b * 8 + a] = value[0]
                stage[1, b * 8 + a] = value[1]
        for b in range(8):
            for t, value in enumerate(dft8([(stage[0, b * 8 + a], stage[1, b * 8 + a]) for a in range(8)])):
                n = b + 8 * t
                c, s = twist[0, n : n + 1, :], twist[1, n : n + 1, :]
                at = pl.ds(n * 32 + part * 16, 16)
                lines[at, 0:128] = (value[0] * c - value[1] * s).astype(jnp.bfloat16)
                lines[at, 128:256] = (value[0] * s + value[1] * c).astype(jnp.bfloat16)
        return carry

    lax.fori_loop(0, 2, one, 0)


def y_squares(sources, matrix, twist, stage, lines, add):
    y_lines(sources, twist, stage, lines)
    for chunk in range(8):
        got = lax.dot_general(
            matrix[...], lines[pl.ds(chunk * 256, 256), :], NT, preferred_element_type=jnp.float32
        )
        got = got[0:128] + got[128:256]
        add((slice(None), slice(chunk * 256, chunk * 256 + 256)), got * got)


def y_first(own, came, matrix, twist, out, stage, lines):
    def add(at, square):
        out[at] = 1.0 + square

    y_squares(((own, 0), (came, 0)), matrix, twist, stage, lines, add)


def y_next(source, before, matrix, twist, out, stage, lines):
    def add(at, square):
        out[at] = before[at] + square

    y_squares(((source, 0), (source, 64)), matrix, twist, stage, lines, add)


def y_last(source, before, matrix, twist, out, stage, lines, total):
    def add(at, square):
        total[at] = jnp.sqrt(before[at] + square)

    y_squares(((source, 128), (source, 192)), matrix, twist, stage, lines, add)

    def put(h, tile, value):
        value = value.astype(jnp.bfloat16)
        for c in range(4):
            for z in range(2):
                out[z * 4 + c, h * 16 : h * 16 + 16, tile * 128 : tile * 128 + 128] = value[c * 16 : c * 16 + 16]

    for h in range(2):
        rows = slice(h * 64, h * 64 + 64)
        for tile in range(16):
            put(h, tile + 1, total[rows, tile * 128 : tile * 128 + 128])
        put(h, 0, pltpu.roll(total[rows, 15 * 128 : 16 * 128], 1, 0))
        put(h, 17, pltpu.roll(total[rows, 0:128], 63, 0))


def y_transform(kernel, sources, y_matrix, y_twist):
    last = kernel is y_last
    sums = jax.ShapeDtypeStruct((128, 2048), jnp.float32)
    scratch = [pltpu.VMEM((2, 64, 16, 128), jnp.float32), pltpu.VMEM((2048, 256), jnp.bfloat16)]
    return pl.pallas_call(
        kernel,
        out_shape=jax.ShapeDtypeStruct((8, 32, 2304), jnp.bfloat16) if last else sums,
        scratch_shapes=scratch + ([pltpu.VMEM((128, 2048), jnp.float32)] if last else []),
        compiler_params=pltpu.CompilerParams(vmem_limit_bytes=VMEM_LIMIT),
        cost_estimate=pl.CostEstimate(flops=2**28, bytes_accessed=2**22, transcendentals=0),
        name=kernel.__name__,
    )(*sources, y_matrix, y_twist)


def smooth_coefficients():
    w = RELAX
    even = np.polynomial.polynomial.polypow([1 - 6 * w + 2 * w, w], 3)
    odd = np.polynomial.polynomial.polypow([1 - 6 * w - 2 * w, w], 3)
    return (even + odd) / 2, (even - odd) / 2


def regroup_kernel(field, own, other):
    me = lax.axis_index("gz")
    lane = lax.broadcasted_iota(jnp.int32, (16, 128), 1)

    def swapped(a, b, width):
        upper = (lane & width) != 0
        return (
            jnp.where(upper, pltpu.roll(b, width, 1), a),
            jnp.where(upper, b, pltpu.roll(a, 128 - width, 1)),
        )

    def regroup(z, target, tile):
        at = pl.ds(pl.multiple_of(tile * 128, 128), 128)
        for ch in range(2):
            v = {
                (c, h): field[z * 4 + ch * 2 + c, h * 16 : h * 16 + 16, at].astype(jnp.float32)
                for c in range(2)
                for h in range(2)
            }
            p = {}
            for h in range(2):
                p[0, h], p[1, h] = swapped(v[0, h], v[1, h], 64)
            for y1 in range(2):
                s0, s1 = swapped(p[y1, 0], p[y1, 1], 16)
                y00, y01 = swapped(s0, s1, 32)
                target[tile * 4 + y1 * 2, :, ch * 128 : ch * 128 + 128] = y00
                target[tile * 4 + y1 * 2 + 1, :, ch * 128 : ch * 128 + 128] = y01

    def both(step, carry):
        for t in range(3):
            regroup(me, own, step * 3 + t)
            regroup(1 - me, other, step * 3 + t)
        return carry

    lax.fori_loop(0, 6, both, 0)


def regroup(field):
    return pl.pallas_call(
        regroup_kernel,
        out_shape=[jax.ShapeDtypeStruct((72, 16, 256), jnp.float32)] * 2,
        compiler_params=pltpu.CompilerParams(vmem_limit_bytes=VMEM_LIMIT),
        cost_estimate=pl.CostEstimate(flops=2**24, bytes_accessed=2**23, transcendentals=0),
        name="regroup",
    )(field)


def edge_kernel(field, low, high):
    lane = lax.broadcasted_iota(jnp.int32, (16, 128), 1)
    for z in range(2):
        for group in range(5):
            last = first = jnp.zeros((16, 128), jnp.float32)
            for t in range(min(4, 18 - group * 4)):
                at = slice((group * 4 + t) * 128, (group * 4 + t) * 128 + 128)
                here = (lane & 24) == 8 * t
                last = jnp.where(here, pltpu.roll(field[z * 4 + 3, 16:32, at].astype(jnp.float32), 100 + 8 * t, 1), last)
                first = jnp.where(here, pltpu.roll(field[z * 4, 0:16, at].astype(jnp.float32), 4 + 8 * t, 1), first)
            low[z, :, group * 128 : group * 128 + 128] = last.astype(jnp.bfloat16)
            high[z, :, group * 128 : group * 128 + 128] = first.astype(jnp.bfloat16)


def edges(field):
    return pl.pallas_call(
        edge_kernel,
        out_shape=[jax.ShapeDtypeStruct((2, 16, 640), jnp.bfloat16)] * 2,
        compiler_params=pltpu.CompilerParams(vmem_limit_bytes=VMEM_LIMIT),
        name="edges",
    )(field)


def smooth_kernel(own, other, low, high, out, own_edge, other_edge, work, spread):
    own_c, other_c = [[float(v) for v in part] for part in smooth_coefficients()]
    me = lax.axis_index("gz")
    lane = lax.broadcasted_iota(jnp.int32, (16, 128), 1)
    is_low = (lane & 7) < 4

    def spread_edges(group, tiles):
        at = pl.ds(pl.multiple_of(group * 128, 128), 128)
        for z, target in ((me, own_edge), (1 - me, other_edge)):
            both = jnp.where(is_low, low[z, :, at].astype(jnp.float32), high[z, :, at].astype(jnp.float32))
            for t in range(tiles):
                for y in range(4):
                    target[(group * 4 + t) * 4 + y] = pltpu.roll(both, 124 - 32 * y - 8 * t, 1)

    def edge_group(group, carry):
        spread_edges(group, 4)
        return carry

    lax.fori_loop(0, 4, edge_group, 0)
    spread_edges(4, 2)

    def beside(ref, y, center):
        sides = pltpu.roll(center, 1, 1) + pltpu.roll(center, 383, 1)
        return sides + (ref(y - 1) + ref(y + 1))

    def own_at(y):
        return jnp.concatenate([own[y], own_edge[y]], axis=1)

    def other_at(y):
        return jnp.concatenate([other[y], other_edge[y]], axis=1)

    def each(begin, end, unroll, body):
        def some(step, carry):
            for t in range(unroll):
                body(begin + step * unroll + t)
            return carry

        lax.fori_loop(0, (end - begin) // unroll, some, 0)

    def first(y):
        center = own_at(y)
        work[0, y] = center * own_c[2] + other_at(y) * other_c[2] + beside(own_at, y, center) * own_c[3]

    def second(y):
        center = work[0, y]
        work[1, y] = own_at(y) * own_c[1] + other_at(y) * other_c[1] + beside(lambda i: work[0, i], y, center)

    def third(y):
        center = work[1, y]
        value = beside(lambda i: work[1, i], y, center)[:, 0:256]
        value = own[y] * own_c[0] + other[y] * other_c[0] + value
        for half in range(2):
            spread[pl.ds(half * 1024 + y - 4, 16, stride=64), :] = value[:, half * 128 : half * 128 + 128]

    each(2, 70, 4, first)
    each(3, 69, 6, second)
    each(4, 68, 4, third)
    for half in range(2):
        out[0, :, half * 128 : half * 128 + 128] = spread[pl.ds(half * 1024, 1024), :]


def smooth(own, other, low, high):
    return pl.pallas_call(
        smooth_kernel,
        out_shape=jax.ShapeDtypeStruct((1, 1024, 256), jnp.float32),
        scratch_shapes=[
            pltpu.VMEM((72, 16, 128), jnp.float32),
            pltpu.VMEM((72, 16, 128), jnp.float32),
            pltpu.VMEM((2, 72, 16, 384), jnp.float32),
            pltpu.VMEM((2048, 128), jnp.float32),
        ],
        compiler_params=pltpu.CompilerParams(vmem_limit_bytes=VMEM_LIMIT),
        name="smooth",
    )(own, other, low, high)


def ring(value, axis, steps):
    count = lax.axis_size(axis)
    return lax.ppermute(value, axis, [(i, (i + steps) % count) for i in range(count)])


def between_y(value, target):
    pairs = []
    for y_hi in range(2):
        for gz in range(2):
            to_hi, to_gz = target(y_hi, gz)
            pairs.append((y_hi * 2 + gz, to_hi * 2 + to_gz))
    return lax.ppermute(value, ("yh", "gz"), pairs)


def shards(velocity_hat):
    x_matrix, x_twist, y_matrix, y_twist = (jnp.asarray(t) for t in tables())
    parts = velocity_hat.reshape((3, 2) + velocity_hat.shape[3:])

    def exchanged(array, axes):
        return lax.all_to_all(array, axes, split_axis=0, concat_axis=0, tiled=True)

    def lines(fields, after=()):
        return x_transform(fields, parts, x_matrix, x_twist, after)

    curl_own, curl_other = lines(("curl_x", "curl_y"))
    curl_z = lines(("curl_z",), (curl_own,))[0]
    term_own, term_other = lines(("u", "v"), (curl_z,))
    came = between_y(curl_other, lambda y_hi, gz: (1 - y_hi, gz))
    near = between_y(term_own, lambda y_hi, gz: (y_hi, 1 - gz))
    across = between_y(term_other, lambda y_hi, gz: (1 - y_hi, 1 - gz))
    line_2 = exchanged(curl_z, ("zc", "col"))
    came_2 = between_y(line_2[:, 64:], lambda y_hi, gz: (1 - y_hi, gz))
    both = exchanged(meet(curl_own, came, near, across), ("zc", "col"))
    squares = y_transform(y_first, (line_2, came_2), y_matrix, y_twist)
    squares = y_transform(y_next, (both, squares), y_matrix, y_twist)
    magnitude = y_transform(y_last, (both, squares), y_matrix, y_twist)
    field = exchanged(magnitude, ("gz", "col"))
    last, first = edges(field)
    low, high = ring(last, ("yh", "zc"), 1), ring(first, ("yh", "zc"), -1)
    own, other = regroup(field)
    return smooth(own, other, low, high)


def solution(mesh):
    rows, cols, planes = mesh.devices.shape
    split = jax.sharding.Mesh(mesh.devices.reshape(2, rows // 2, cols, planes), ("yh", "zc", "col", "gz"))
    return jax.shard_map(
        shards,
        mesh=split,
        in_specs=(P(None, None, "gz", ("yh", "zc", "col"), None),),
        out_specs=P("gz", "col", ("yh", "zc")),
        check_vma=False,
    )
```

```python
import math

import jax
import jax.numpy as jnp
import numpy as np
from jax import lax
from jax.experimental import pallas as pl
from jax.experimental.pallas import tpu as pltpu
from jax.sharding import PartitionSpec as P

GRID = 4096
RELAX = 0.15
VMEM_LIMIT = 28 * 1024 * 1024
PAD = 72
NT = (((1,), (1,)), ((), ()))


def cos_sin(rows, columns, period):
    turn = rows[:, None] * columns[None, :] % period
    angle = turn.astype(jnp.float32) * (2.0 * math.pi / period)
    return jnp.cos(angle), jnp.sin(angle)


def split_bf16(table):
    high = table.astype(jnp.bfloat16)
    low = (table - high.astype(jnp.float32)).astype(jnp.bfloat16)
    return jnp.concatenate([high, low], axis=0)


def tables():
    k, j, b = jnp.arange(128), jnp.arange(64), jnp.arange(64)
    blocks = []
    for s in range(2):
        c, d = cos_sin(b * 2 + s, k, 128)
        blocks.append(jnp.concatenate([c, -d], axis=1))
        blocks.append(jnp.concatenate([d, c], axis=1))
    x_matrix = split_bf16(jnp.concatenate(blocks, axis=0))
    x_twist = jnp.stack(cos_sin(jnp.arange(32), k, 4096)) / 64
    zero = jnp.zeros((64, 64), jnp.float32)
    c, d = cos_sin(j, j, 64)
    y_matrix = split_bf16(
        jnp.concatenate(
            [jnp.concatenate([c, zero, -d, zero], axis=1), jnp.concatenate([zero, c, zero, -d], axis=1)], axis=0
        )
    )
    y_twist = jnp.stack(cos_sin(j, j, 4096)) / 64
    return x_matrix, x_twist, y_matrix, jnp.concatenate([y_twist, y_twist], axis=2)


def turned(value, num, den):
    re, im = value
    num = num % den
    if num == 0:
        return value
    if 2 * num == den:
        return (-re, -im)
    if 4 * num == den:
        return (-im, re)
    if 4 * num == 3 * den:
        return (im, -re)
    if 8 * num == den:
        r = math.sqrt(0.5)
        return ((re - im) * r, (re + im) * r)
    if 8 * num == 3 * den:
        r = math.sqrt(0.5)
        return ((re + im) * -r, (re - im) * r)
    c, s = math.cos(2 * math.pi * num / den), math.sin(2 * math.pi * num / den)
    return (re * c - im * s, re * s + im * c)


def plus(a, b):
    return (a[0] + b[0], a[1] + b[1])


def minus(a, b):
    return (a[0] - b[0], a[1] - b[1])


def dft4(v):
    a, b = plus(v[0], v[2]), minus(v[0], v[2])
    c, d = plus(v[1], v[3]), minus(v[1], v[3])
    return [plus(a, c), (b[0] - d[1], b[1] + d[0]), minus(a, c), (b[0] + d[1], b[1] - d[0])]


def dft8(v):
    even, odd = dft4(v[0::2]), dft4(v[1::2])
    odd = [turned(odd[t], t, 8) for t in range(4)]
    return [plus(e, o) for e, o in zip(even, odd)] + [minus(e, o) for e, o in zip(even, odd)]


def x_kernel(fields, rows_local, *refs):
    n_in = 2 if fields == ("curl_z",) or fields[0] == "u" else 3
    n_out = 2 if len(fields) == 2 else 1
    ins, (matrix, twist), refs = refs[:n_in], refs[n_in : n_in + 2], refs[n_in + 2 :]
    outs, (stage, lines, spread) = refs[-3 - n_out : -3], refs[-3:]
    step = pl.program_id(0)
    scale = 2.0 * math.pi / GRID
    lane = lax.broadcasted_iota(jnp.int32, (16, 128), 1)
    row = lax.broadcasted_iota(jnp.int32, (16, 128), 0)
    start = lax.axis_index(("yh", "zc", "col")) * rows_local + step * 16
    ky = row + start
    wave_y = jnp.where(ky >= GRID // 2, ky - GRID, ky).astype(jnp.float32) * scale

    def tile(ref, part, q):
        return ref[0, part, :, pl.ds(q * 128, 128)].astype(jnp.float32)

    def wave_x(q):
        base = q * 128 - (GRID if q >= 16 else 0)
        return (lane + base).astype(jnp.float32) * scale

    def value_of(field, q):
        if field == "curl_z":
            u, v = ins
            wx = wave_x(q)
            return (
                wave_y * tile(u, 1, q) - wx * tile(v, 1, q),
                wx * tile(v, 0, q) - wave_y * tile(u, 0, q),
            )
        if field == "u":
            return (tile(ins[0], 0, q), tile(ins[0], 1, q))
        if field == "v":
            return (tile(ins[1], 0, q), tile(ins[1], 1, q))
        u, v, w = ins
        if field == "curl_x":
            return (tile(v, 0, q) - wave_y * tile(w, 1, q), tile(v, 1, q) + wave_y * tile(w, 0, q))
        wx = wave_x(q)
        return (wx * tile(w, 1, q) - tile(u, 0, q), -wx * tile(w, 0, q) - tile(u, 1, q))

    for index, field in enumerate(fields):
        for a in range(8):
            for b, value in enumerate(dft4([value_of(field, a + 8 * t) for t in range(4)])):
                value = turned(value, a * b, 32)
                stage[0, b * 8 + a] = value[0]
                stage[1, b * 8 + a] = value[1]
        for b in range(4):
            for t, value in enumerate(dft8([(stage[0, b * 8 + a], stage[1, b * 8 + a]) for a in range(8)])):
                n = b + 4 * t
                c, s = twist[0, n : n + 1, :], twist[1, n : n + 1, :]
                at = pl.ds(((n % 16) * 2 + n // 16) * 64 + step * 16, 16)
                lines[index, at, 0:128] = (value[0] * c - value[1] * s).astype(jnp.bfloat16)
                lines[index, at, 128:256] = (value[0] * s + value[1] * c).astype(jnp.bfloat16)

    @pl.when(step == 3)
    def _():
        for index in range(len(fields)):
            for pair in range(8):
                got = lax.dot_general(
                    matrix[...], lines[index, pl.ds(pair * 256, 256), :], NT, preferred_element_type=jnp.float32
                )
                got = got[0:256] + got[256:512]
                for half in range(2):
                    n16 = pair * 2 + half
                    for s in range(2):
                        for c in range(2):
                            at = (s * 2 + c) * 64
                            spread[pl.ds(c * 32 + s * 16 + n16, 64, stride=PAD), :] = got[
                                at : at + 64, half * 128 : half * 128 + 128
                            ]
            for half in range(2):
                first = (lax.axis_index("yh") + half) % 2 * (32 * PAD)
                for b in range(32):
                    at = pl.ds(pl.multiple_of(first + b * PAD, 8), 64)
                    block = spread[at, :].astype(jnp.bfloat16)
                    if n_out == 1:
                        outs[0][b, half * 64 : half * 64 + 64, :] = block
                    else:
                        outs[half][b, index * 64 : index * 64 + 64, :] = block


def x_transform(fields, parts, x_matrix, x_twist, after=()):
    rows_local = parts.shape[2]
    comps = (0, 1, 2) if fields[0] == "curl_x" else (0, 1)
    specs = [pl.BlockSpec((1, 2, 16, GRID), lambda i, comp=comp: (comp, 0, i, 0)) for comp in comps] + [
        pl.BlockSpec((512, 256), lambda i: (0, 0)),
        pl.BlockSpec((2, 32, 128), lambda i: (0, 0, 0)),
    ]
    specs += [pl.BlockSpec(memory_space=pl.ANY)] * len(after)
    return pl.pallas_call(
        lambda *refs: x_kernel(fields, rows_local, *refs),
        grid=(rows_local // 16,),
        in_specs=specs,
        out_specs=[pl.BlockSpec((32, 128, 128), lambda i: (0, 0, 0))] * len(fields),
        out_shape=[jax.ShapeDtypeStruct((32, 128, 128), jnp.bfloat16)] * len(fields),
        scratch_shapes=[
            pltpu.VMEM((2, 32, 16, 128), jnp.float32),
            pltpu.VMEM((len(fields), 2048, 256), jnp.bfloat16),
            pltpu.VMEM((64 * PAD, 128), jnp.float32),
        ],
        compiler_params=pltpu.CompilerParams(vmem_limit_bytes=VMEM_LIMIT),
        cost_estimate=pl.CostEstimate(flops=2**30, bytes_accessed=2**22, transcendentals=0),
        name="lines_" + "_".join(fields),
    )(*[parts] * len(comps), x_matrix, x_twist, *after)


def meet_kernel(own, came, near, across, out):
    for b in range(out.shape[0]):
        for index, sign in ((0, -1.0), (1, 1.0)):
            rows, term_rows = slice(index * 64, index * 64 + 64), slice(64 - index * 64, 128 - index * 64)
            for half, (field, term) in enumerate(((own, near), (came, across))):
                value = field[b, rows, :].astype(jnp.float32) + sign * term[b, term_rows, :].astype(jnp.float32)
                at = index * 128 + half * 64
                out[b, at : at + 64, :] = value.astype(jnp.bfloat16)


def meet(own, came, near, across):
    return pl.pallas_call(
        meet_kernel,
        grid=(2,),
        in_specs=[pl.BlockSpec((16, 128, 128), lambda i: (i, 0, 0))] * 4,
        out_specs=pl.BlockSpec((16, 256, 128), lambda i: (i, 0, 0)),
        out_shape=jax.ShapeDtypeStruct((32, 256, 128), jnp.bfloat16),
        compiler_params=pltpu.CompilerParams(vmem_limit_bytes=VMEM_LIMIT),
        cost_estimate=pl.CostEstimate(flops=2**20, bytes_accessed=2**22, transcendentals=0),
        name="meet",
    )(own, came, near, across)


def y_lines(sources, twist, stage, lines):
    def one(part, carry):
        def load(c, d):
            source, first = sources[d // 32]
            return source[d % 32, pl.ds(first + c * 32 + part * 16, 16), :].astype(jnp.float32)

        for a in range(8):
            values = [(load(0, a + 8 * t), load(1, a + 8 * t)) for t in range(8)]
            for b, value in enumerate(dft8(values)):
                value = turned(value, a * b, 64)
                stage[0, b * 8 + a] = value[0]
                stage[1, b * 8 + a] = value[1]
        for b in range(8):
            for t, value in enumerate(dft8([(stage[0, b * 8 + a], stage[1, b * 8 + a]) for a in range(8)])):
                n = b + 8 * t
                c, s = twist[0, n : n + 1, :], twist[1, n : n + 1, :]
                at = pl.ds(n * 32 + part * 16, 16)
                lines[at, 0:128] = (value[0] * c - value[1] * s).astype(jnp.bfloat16)
                lines[at, 128:256] = (value[0] * s + value[1] * c).astype(jnp.bfloat16)
        return carry

    lax.fori_loop(0, 2, one, 0)


def y_squares(sources, matrix, twist, stage, lines, add):
    y_lines(sources, twist, stage, lines)
    for chunk in range(8):
        got = lax.dot_general(
            matrix[...], lines[pl.ds(chunk * 256, 256), :], NT, preferred_element_type=jnp.float32
        )
        got = got[0:128] + got[128:256]
        add((slice(None), slice(chunk * 256, chunk * 256 + 256)), got * got)


def y_first(own, came, matrix, twist, out, stage, lines):
    def add(at, square):
        out[at] = 1.0 + square

    y_squares(((own, 0), (came, 0)), matrix, twist, stage, lines, add)


def y_last(source, before, matrix, twist, out, stage, lines, total):
    def add(at, square):
        total[at] = before[at] + square

    def finish(at, square):
        total[at] = jnp.sqrt(total[at] + square)

    y_squares(((source, 0), (source, 64)), matrix, twist, stage, lines, add)
    y_squares(((source, 128), (source, 192)), matrix, twist, stage, lines, finish)

    def put(h, tile, value):
        value = value.astype(jnp.bfloat16)
        for c in range(4):
            for z in range(2):
                out[z * 4 + c, h * 16 : h * 16 + 16, tile * 128 : tile * 128 + 128] = value[c * 16 : c * 16 + 16]

    for h in range(2):
        rows = slice(h * 64, h * 64 + 64)
        for tile in range(16):
            put(h, tile + 1, total[rows, tile * 128 : tile * 128 + 128])
        put(h, 0, pltpu.roll(total[rows, 15 * 128 : 16 * 128], 1, 0))
        put(h, 17, pltpu.roll(total[rows, 0:128], 63, 0))


def y_transform(kernel, sources, y_matrix, y_twist):
    last = kernel is y_last
    sums = jax.ShapeDtypeStruct((128, 2048), jnp.float32)
    scratch = [pltpu.VMEM((2, 64, 16, 128), jnp.float32), pltpu.VMEM((2048, 256), jnp.bfloat16)]
    return pl.pallas_call(
        kernel,
        out_shape=jax.ShapeDtypeStruct((8, 32, 2304), jnp.bfloat16) if last else sums,
        scratch_shapes=scratch + ([pltpu.VMEM((128, 2048), jnp.float32)] if last else []),
        compiler_params=pltpu.CompilerParams(vmem_limit_bytes=VMEM_LIMIT),
        cost_estimate=pl.CostEstimate(flops=2**28, bytes_accessed=2**22, transcendentals=0),
        name=kernel.__name__,
    )(*sources, y_matrix, y_twist)


def smooth_coefficients():
    w = RELAX
    even = np.polynomial.polynomial.polypow([1 - 6 * w + 2 * w, w], 3)
    odd = np.polynomial.polynomial.polypow([1 - 6 * w - 2 * w, w], 3)
    return (even + odd) / 2, (even - odd) / 2


def regroup_kernel(field, own, other):
    me = lax.axis_index("gz")
    lane = lax.broadcasted_iota(jnp.int32, (16, 128), 1)

    def swapped(a, b, width):
        upper = (lane & width) != 0
        return (
            jnp.where(upper, pltpu.roll(b, width, 1), a),
            jnp.where(upper, b, pltpu.roll(a, 128 - width, 1)),
        )

    def regroup(z, target, tile):
        at = pl.ds(pl.multiple_of(tile * 128, 128), 128)
        for ch in range(2):
            v = {
                (c, h): field[z * 4 + ch * 2 + c, h * 16 : h * 16 + 16, at].astype(jnp.float32)
                for c in range(2)
                for h in range(2)
            }
            p = {}
            for h in range(2):
                p[0, h], p[1, h] = swapped(v[0, h], v[1, h], 64)
            for y1 in range(2):
                s0, s1 = swapped(p[y1, 0], p[y1, 1], 16)
                y00, y01 = swapped(s0, s1, 32)
                target[tile * 4 + y1 * 2, :, ch * 128 : ch * 128 + 128] = y00
                target[tile * 4 + y1 * 2 + 1, :, ch * 128 : ch * 128 + 128] = y01

    def both(step, carry):
        for t in range(3):
            regroup(me, own, step * 3 + t)
            regroup(1 - me, other, step * 3 + t)
        return carry

    lax.fori_loop(0, 6, both, 0)


def regroup(field):
    return pl.pallas_call(
        regroup_kernel,
        out_shape=[jax.ShapeDtypeStruct((72, 16, 256), jnp.float32)] * 2,
        compiler_params=pltpu.CompilerParams(vmem_limit_bytes=VMEM_LIMIT),
        cost_estimate=pl.CostEstimate(flops=2**24, bytes_accessed=2**23, transcendentals=0),
        name="regroup",
    )(field)


def edge_kernel(field, low, high):
    lane = lax.broadcasted_iota(jnp.int32, (16, 128), 1)
    for z in range(2):
        for group in range(5):
            last = first = jnp.zeros((16, 128), jnp.float32)
            for t in range(min(4, 18 - group * 4)):
                at = slice((group * 4 + t) * 128, (group * 4 + t) * 128 + 128)
                here = (lane & 24) == 8 * t
                last = jnp.where(here, pltpu.roll(field[z * 4 + 3, 16:32, at].astype(jnp.float32), 100 + 8 * t, 1), last)
                first = jnp.where(here, pltpu.roll(field[z * 4, 0:16, at].astype(jnp.float32), 4 + 8 * t, 1), first)
            low[z, :, group * 128 : group * 128 + 128] = last.astype(jnp.bfloat16)
            high[z, :, group * 128 : group * 128 + 128] = first.astype(jnp.bfloat16)


def edges(field):
    return pl.pallas_call(
        edge_kernel,
        out_shape=[jax.ShapeDtypeStruct((2, 16, 640), jnp.bfloat16)] * 2,
        compiler_params=pltpu.CompilerParams(vmem_limit_bytes=VMEM_LIMIT),
        name="edges",
    )(field)


def smooth_kernel(own, other, low, high, out, own_edge, other_edge, work, spread):
    own_c, other_c = [[float(v) for v in part] for part in smooth_coefficients()]
    me = lax.axis_index("gz")
    lane = lax.broadcasted_iota(jnp.int32, (16, 128), 1)
    is_low = (lane & 7) < 4

    def spread_edges(group, tiles):
        at = pl.ds(pl.multiple_of(group * 128, 128), 128)
        for z, target in ((me, own_edge), (1 - me, other_edge)):
            both = jnp.where(is_low, low[z, :, at].astype(jnp.float32), high[z, :, at].astype(jnp.float32))
            for t in range(tiles):
                for y in range(4):
                    target[(group * 4 + t) * 4 + y] = pltpu.roll(both, 124 - 32 * y - 8 * t, 1)

    def edge_group(group, carry):
        spread_edges(group, 4)
        return carry

    lax.fori_loop(0, 4, edge_group, 0)
    spread_edges(4, 2)

    def beside(ref, y, center):
        sides = pltpu.roll(center, 1, 1) + pltpu.roll(center, 383, 1)
        return sides + (ref(y - 1) + ref(y + 1))

    def own_at(y):
        return jnp.concatenate([own[y], own_edge[y]], axis=1)

    def other_at(y):
        return jnp.concatenate([other[y], other_edge[y]], axis=1)

    def each(begin, end, unroll, body):
        def some(step, carry):
            for t in range(unroll):
                body(begin + step * unroll + t)
            return carry

        lax.fori_loop(0, (end - begin) // unroll, some, 0)

    def first(y):
        center = own_at(y)
        work[0, y] = center * own_c[2] + other_at(y) * other_c[2] + beside(own_at, y, center) * own_c[3]

    def second(y):
        center = work[0, y]
        work[1, y] = own_at(y) * own_c[1] + other_at(y) * other_c[1] + beside(lambda i: work[0, i], y, center)

    def third(y):
        center = work[1, y]
        value = beside(lambda i: work[1, i], y, center)[:, 0:256]
        value = own[y] * own_c[0] + other[y] * other_c[0] + value
        for half in range(2):
            spread[pl.ds(half * 16 * PAD + y - 4, 16, stride=PAD), :] = value[:, half * 128 : half * 128 + 128]

    each(2, 70, 34, first)
    each(3, 69, 33, second)
    each(4, 68, 32, third)
    for half in range(2):
        for k in range(16):
            out[0, k * 64 : k * 64 + 64, half * 128 : half * 128 + 128] = spread[pl.ds((half * 16 + k) * PAD, 64), :]


def smooth(own, other, low, high):
    return pl.pallas_call(
        smooth_kernel,
        out_shape=jax.ShapeDtypeStruct((1, 1024, 256), jnp.float32),
        scratch_shapes=[
            pltpu.VMEM((72, 16, 128), jnp.float32),
            pltpu.VMEM((72, 16, 128), jnp.float32),
            pltpu.VMEM((2, 72, 16, 384), jnp.float32),
            pltpu.VMEM((32 * PAD, 128), jnp.float32),
        ],
        compiler_params=pltpu.CompilerParams(vmem_limit_bytes=VMEM_LIMIT),
        name="smooth",
    )(own, other, low, high)


def ring(value, axis, steps):
    count = lax.axis_size(axis)
    return lax.ppermute(value, axis, [(i, (i + steps) % count) for i in range(count)])


def between_y(value, target):
    pairs = []
    for y_hi in range(2):
        for gz in range(2):
            to_hi, to_gz = target(y_hi, gz)
            pairs.append((y_hi * 2 + gz, to_hi * 2 + to_gz))
    return lax.ppermute(value, ("yh", "gz"), pairs)


def shards(velocity_hat):
    x_matrix, x_twist, y_matrix, y_twist = tables()
    parts = velocity_hat.reshape((3, 2) + velocity_hat.shape[3:])

    def exchanged(array, axes):
        return lax.all_to_all(array, axes, split_axis=0, concat_axis=0, tiled=True)

    def lines(fields, after=()):
        return x_transform(fields, parts, x_matrix, x_twist, after)

    curl_own, curl_other = lines(("curl_x", "curl_y"))
    curl_z = lines(("curl_z",), (curl_own,))[0]
    term_own, term_other = lines(("u", "v"), (curl_z,))
    came = between_y(curl_other, lambda y_hi, gz: (1 - y_hi, gz))
    near = between_y(term_own, lambda y_hi, gz: (y_hi, 1 - gz))
    across = between_y(term_other, lambda y_hi, gz: (1 - y_hi, 1 - gz))
    line_2 = exchanged(curl_z, ("zc", "col"))
    came_2 = between_y(line_2[:, 64:], lambda y_hi, gz: (1 - y_hi, gz))
    both = exchanged(meet(curl_own, came, near, across), ("zc", "col"))
    squares = y_transform(y_first, (line_2, came_2), y_matrix, y_twist)
    magnitude = y_transform(y_last, (both, squares), y_matrix, y_twist)
    field = exchanged(magnitude, ("gz", "col"))
    last, first = edges(field)
    low, high = ring(last, ("yh", "zc"), 1), ring(first, ("yh", "zc"), -1)
    own, other = regroup(field)
    return smooth(own, other, low, high)


def solution(mesh):
    rows, cols, planes = mesh.devices.shape
    split = jax.sharding.Mesh(mesh.devices.reshape(2, rows // 2, cols, planes), ("yh", "zc", "col", "gz"))
    return jax.shard_map(
        shards,
        mesh=split,
        in_specs=(P(None, None, "gz", ("yh", "zc", "col"), None),),
        out_specs=P("gz", "col", ("yh", "zc")),
        check_vma=False,
    )
```

```python
import math

import jax
import jax.numpy as jnp
import numpy as np
from jax import lax
from jax.experimental import pallas as pl
from jax.experimental.pallas import tpu as pltpu
from jax.sharding import PartitionSpec as P

GRID = 4096
RELAX = 0.15
VMEM_LIMIT = 28 * 1024 * 1024
PAD = 72
NT = (((1,), (1,)), ((), ()))


def cos_sin(rows, columns, period):
    turn = rows[:, None] * columns[None, :] % period
    angle = turn.astype(jnp.float32) * (2.0 * math.pi / period)
    return jnp.cos(angle), jnp.sin(angle)


def split_bf16(table):
    high = lax.reduce_precision(table, exponent_bits=8, mantissa_bits=7)
    return jnp.concatenate([high, table - high], axis=0).astype(jnp.bfloat16)


def tables():
    k, j, b = jnp.arange(128), jnp.arange(64), jnp.arange(64)
    blocks = []
    for s in range(2):
        c, d = cos_sin(b * 2 + s, k, 128)
        blocks.append(jnp.concatenate([c, -d], axis=1))
        blocks.append(jnp.concatenate([d, c], axis=1))
    x_matrix = split_bf16(jnp.concatenate(blocks, axis=0))
    x_twist = jnp.stack(cos_sin(jnp.arange(32), k, 4096)) / 64
    zero = jnp.zeros((64, 64), jnp.float32)
    c, d = cos_sin(j, j, 64)
    y_matrix = split_bf16(
        jnp.concatenate(
            [jnp.concatenate([c, zero, -d, zero], axis=1), jnp.concatenate([zero, c, zero, -d], axis=1)], axis=0
        )
    )
    y_twist = jnp.stack(cos_sin(j, j, 4096)) / 64
    return x_matrix, x_twist, y_matrix, jnp.concatenate([y_twist, y_twist], axis=2)


def turned(value, num, den):
    re, im = value
    num = num % den
    if num == 0:
        return value
    if 2 * num == den:
        return (-re, -im)
    if 4 * num == den:
        return (-im, re)
    if 4 * num == 3 * den:
        return (im, -re)
    if 8 * num == den:
        r = math.sqrt(0.5)
        return ((re - im) * r, (re + im) * r)
    if 8 * num == 3 * den:
        r = math.sqrt(0.5)
        return ((re + im) * -r, (re - im) * r)
    c, s = math.cos(2 * math.pi * num / den), math.sin(2 * math.pi * num / den)
    return (re * c - im * s, re * s + im * c)


def plus(a, b):
    return (a[0] + b[0], a[1] + b[1])


def minus(a, b):
    return (a[0] - b[0], a[1] - b[1])


def dft4(v):
    a, b = plus(v[0], v[2]), minus(v[0], v[2])
    c, d = plus(v[1], v[3]), minus(v[1], v[3])
    return [plus(a, c), (b[0] - d[1], b[1] + d[0]), minus(a, c), (b[0] + d[1], b[1] - d[0])]


def dft8(v):
    even, odd = dft4(v[0::2]), dft4(v[1::2])
    odd = [turned(odd[t], t, 8) for t in range(4)]
    return [plus(e, o) for e, o in zip(even, odd)] + [minus(e, o) for e, o in zip(even, odd)]


def x_kernel(fields, rows_local, *refs):
    n_in = 2 if fields == ("curl_z",) or fields[0] == "u" else 3
    n_out = 2 if len(fields) == 2 else 1
    ins, (matrix, twist), refs = refs[:n_in], refs[n_in : n_in + 2], refs[n_in + 2 :]
    outs, (stage, lines, spread) = refs[-3 - n_out : -3], refs[-3:]
    step = pl.program_id(0)
    scale = 2.0 * math.pi / GRID
    lane = lax.broadcasted_iota(jnp.int32, (16, 128), 1)
    row = lax.broadcasted_iota(jnp.int32, (16, 128), 0)
    start = lax.axis_index(("yh", "zc", "col")) * rows_local + step * 16
    ky = row + start
    wave_y = jnp.where(ky >= GRID // 2, ky - GRID, ky).astype(jnp.float32) * scale

    def tile(ref, part, q):
        return ref[0, part, :, pl.ds(q * 128, 128)].astype(jnp.float32)

    def wave_x(q):
        base = q * 128 - (GRID if q >= 16 else 0)
        return (lane + base).astype(jnp.float32) * scale

    def value_of(field, q):
        if field == "curl_z":
            u, v = ins
            wx = wave_x(q)
            return (
                wave_y * tile(u, 1, q) - wx * tile(v, 1, q),
                wx * tile(v, 0, q) - wave_y * tile(u, 0, q),
            )
        if field == "u":
            return (tile(ins[0], 0, q), tile(ins[0], 1, q))
        if field == "v":
            return (tile(ins[1], 0, q), tile(ins[1], 1, q))
        u, v, w = ins
        if field == "curl_x":
            return (tile(v, 0, q) - wave_y * tile(w, 1, q), tile(v, 1, q) + wave_y * tile(w, 0, q))
        wx = wave_x(q)
        return (wx * tile(w, 1, q) - tile(u, 0, q), -wx * tile(w, 0, q) - tile(u, 1, q))

    for index, field in enumerate(fields):
        for a in range(8):
            for b, value in enumerate(dft4([value_of(field, a + 8 * t) for t in range(4)])):
                value = turned(value, a * b, 32)
                stage[0, b * 8 + a] = value[0]
                stage[1, b * 8 + a] = value[1]
        for b in range(4):
            for t, value in enumerate(dft8([(stage[0, b * 8 + a], stage[1, b * 8 + a]) for a in range(8)])):
                n = b + 4 * t
                c, s = twist[0, n : n + 1, :], twist[1, n : n + 1, :]
                at = pl.ds(((n % 16) * 2 + n // 16) * 64 + step * 16, 16)
                lines[index, at, 0:128] = (value[0] * c - value[1] * s).astype(jnp.bfloat16)
                lines[index, at, 128:256] = (value[0] * s + value[1] * c).astype(jnp.bfloat16)

    @pl.when(step == 3)
    def _():
        for index in range(len(fields)):
            for pair in range(8):
                got = lax.dot_general(
                    matrix[...], lines[index, pl.ds(pair * 256, 256), :], NT, preferred_element_type=jnp.float32
                )
                got = got[0:256] + got[256:512]
                for half in range(2):
                    n16 = pair * 2 + half
                    for s in range(2):
                        for c in range(2):
                            at = (s * 2 + c) * 64
                            spread[pl.ds(c * 32 + s * 16 + n16, 64, stride=PAD), :] = got[
                                at : at + 64, half * 128 : half * 128 + 128
                            ]
            for half in range(2):
                first = (lax.axis_index("yh") + half) % 2 * (32 * PAD)
                for b in range(32):
                    at = pl.ds(pl.multiple_of(first + b * PAD, 8), 64)
                    block = spread[at, :].astype(jnp.bfloat16)
                    if n_out == 1:
                        outs[0][b, half * 64 : half * 64 + 64, :] = block
                    else:
                        outs[half][b, index * 64 : index * 64 + 64, :] = block


def x_transform(fields, parts, x_matrix, x_twist, after=()):
    rows_local = parts.shape[2]
    comps = (0, 1, 2) if fields[0] == "curl_x" else (0, 1)
    specs = [pl.BlockSpec((1, 2, 16, GRID), lambda i, comp=comp: (comp, 0, i, 0)) for comp in comps] + [
        pl.BlockSpec((512, 256), lambda i: (0, 0)),
        pl.BlockSpec((2, 32, 128), lambda i: (0, 0, 0)),
    ]
    specs += [pl.BlockSpec(memory_space=pl.ANY)] * len(after)
    return pl.pallas_call(
        lambda *refs: x_kernel(fields, rows_local, *refs),
        grid=(rows_local // 16,),
        in_specs=specs,
        out_specs=[pl.BlockSpec((32, 128, 128), lambda i: (0, 0, 0))] * len(fields),
        out_shape=[jax.ShapeDtypeStruct((32, 128, 128), jnp.bfloat16)] * len(fields),
        scratch_shapes=[
            pltpu.VMEM((2, 32, 16, 128), jnp.float32),
            pltpu.VMEM((len(fields), 2048, 256), jnp.bfloat16),
            pltpu.VMEM((64 * PAD, 128), jnp.float32),
        ],
        compiler_params=pltpu.CompilerParams(vmem_limit_bytes=VMEM_LIMIT),
        cost_estimate=pl.CostEstimate(flops=2**30, bytes_accessed=2**22, transcendentals=0),
        name="lines_" + "_".join(fields),
    )(*[parts] * len(comps), x_matrix, x_twist, *after)


def meet_kernel(own, came, near, across, out):
    for b in range(out.shape[0]):
        for index, sign in ((0, -1.0), (1, 1.0)):
            rows, term_rows = slice(index * 64, index * 64 + 64), slice(64 - index * 64, 128 - index * 64)
            for half, (field, term) in enumerate(((own, near), (came, across))):
                value = field[b, rows, :].astype(jnp.float32) + sign * term[b, term_rows, :].astype(jnp.float32)
                at = index * 128 + half * 64
                out[b, at : at + 64, :] = value.astype(jnp.bfloat16)


def meet(own, came, near, across):
    return pl.pallas_call(
        meet_kernel,
        grid=(2,),
        in_specs=[pl.BlockSpec((16, 128, 128), lambda i: (i, 0, 0))] * 4,
        out_specs=pl.BlockSpec((16, 256, 128), lambda i: (i, 0, 0)),
        out_shape=jax.ShapeDtypeStruct((32, 256, 128), jnp.bfloat16),
        compiler_params=pltpu.CompilerParams(vmem_limit_bytes=VMEM_LIMIT),
        cost_estimate=pl.CostEstimate(flops=2**20, bytes_accessed=2**22, transcendentals=0),
        name="meet",
    )(own, came, near, across)


def y_lines(sources, twist, stage, lines):
    def one(part, carry):
        def load(c, d):
            source, first = sources[d // 32]
            return source[d % 32, pl.ds(first + c * 32 + part * 16, 16), :].astype(jnp.float32)

        for a in range(8):
            values = [(load(0, a + 8 * t), load(1, a + 8 * t)) for t in range(8)]
            for b, value in enumerate(dft8(values)):
                value = turned(value, a * b, 64)
                stage[0, b * 8 + a] = value[0]
                stage[1, b * 8 + a] = value[1]
        for b in range(8):
            for t, value in enumerate(dft8([(stage[0, b * 8 + a], stage[1, b * 8 + a]) for a in range(8)])):
                n = b + 8 * t
                c, s = twist[0, n : n + 1, :], twist[1, n : n + 1, :]
                at = pl.ds(n * 32 + part * 16, 16)
                lines[at, 0:128] = (value[0] * c - value[1] * s).astype(jnp.bfloat16)
                lines[at, 128:256] = (value[0] * s + value[1] * c).astype(jnp.bfloat16)
        return carry

    lax.fori_loop(0, 2, one, 0)


def y_squares(sources, matrix, twist, stage, lines, add):
    y_lines(sources, twist, stage, lines)
    for chunk in range(8):
        got = lax.dot_general(
            matrix[...], lines[pl.ds(chunk * 256, 256), :], NT, preferred_element_type=jnp.float32
        )
        got = got[0:128] + got[128:256]
        add((slice(None), slice(chunk * 256, chunk * 256 + 256)), got * got)


def y_first(own, came, matrix, twist, out, stage, lines):
    def add(at, square):
        out[at] = 1.0 + square

    y_squares(((own, 0), (came, 0)), matrix, twist, stage, lines, add)


def y_last(source, before, matrix, twist, out, stage, lines, total):
    def add(at, square):
        total[at] = before[at] + square

    def finish(at, square):
        total[at] = jnp.sqrt(total[at] + square)

    y_squares(((source, 0), (source, 64)), matrix, twist, stage, lines, add)
    y_squares(((source, 128), (source, 192)), matrix, twist, stage, lines, finish)

    def put(h, tile, value):
        value = value.astype(jnp.bfloat16)
        for c in range(4):
            for z in range(2):
                out[z * 4 + c, h * 16 : h * 16 + 16, tile * 128 : tile * 128 + 128] = value[c * 16 : c * 16 + 16]

    for h in range(2):
        rows = slice(h * 64, h * 64 + 64)
        for tile in range(16):
            put(h, tile + 1, total[rows, tile * 128 : tile * 128 + 128])
        put(h, 0, pltpu.roll(total[rows, 15 * 128 : 16 * 128], 1, 0))
        put(h, 17, pltpu.roll(total[rows, 0:128], 63, 0))


def y_transform(kernel, sources, y_matrix, y_twist):
    last = kernel is y_last
    sums = jax.ShapeDtypeStruct((128, 2048), jnp.float32)
    scratch = [pltpu.VMEM((2, 64, 16, 128), jnp.float32), pltpu.VMEM((2048, 256), jnp.bfloat16)]
    return pl.pallas_call(
        kernel,
        out_shape=jax.ShapeDtypeStruct((8, 32, 2304), jnp.bfloat16) if last else sums,
        scratch_shapes=scratch + ([pltpu.VMEM((128, 2048), jnp.float32)] if last else []),
        compiler_params=pltpu.CompilerParams(vmem_limit_bytes=VMEM_LIMIT),
        cost_estimate=pl.CostEstimate(flops=2**28, bytes_accessed=2**22, transcendentals=0),
        name=kernel.__name__,
    )(*sources, y_matrix, y_twist)


def smooth_coefficients():
    w = RELAX
    even = np.polynomial.polynomial.polypow([1 - 6 * w + 2 * w, w], 3)
    odd = np.polynomial.polynomial.polypow([1 - 6 * w - 2 * w, w], 3)
    return (even + odd) / 2, (even - odd) / 2


def regroup_kernel(field, own, other):
    me = lax.axis_index("gz")
    lane = lax.broadcasted_iota(jnp.int32, (16, 128), 1)

    def swapped(a, b, width):
        upper = (lane & width) != 0
        return (
            jnp.where(upper, pltpu.roll(b, width, 1), a),
            jnp.where(upper, b, pltpu.roll(a, 128 - width, 1)),
        )

    def regroup(z, target, tile):
        at = pl.ds(pl.multiple_of(tile * 128, 128), 128)
        for ch in range(2):
            v = {
                (c, h): field[z * 4 + ch * 2 + c, h * 16 : h * 16 + 16, at].astype(jnp.float32)
                for c in range(2)
                for h in range(2)
            }
            p = {}
            for h in range(2):
                p[0, h], p[1, h] = swapped(v[0, h], v[1, h], 64)
            for y1 in range(2):
                s0, s1 = swapped(p[y1, 0], p[y1, 1], 16)
                y00, y01 = swapped(s0, s1, 32)
                target[tile * 4 + y1 * 2, :, ch * 128 : ch * 128 + 128] = y00
                target[tile * 4 + y1 * 2 + 1, :, ch * 128 : ch * 128 + 128] = y01

    def both(step, carry):
        for t in range(3):
            regroup(me, own, step * 3 + t)
            regroup(1 - me, other, step * 3 + t)
        return carry

    lax.fori_loop(0, 6, both, 0)


def regroup(field):
    return pl.pallas_call(
        regroup_kernel,
        out_shape=[jax.ShapeDtypeStruct((72, 16, 256), jnp.float32)] * 2,
        compiler_params=pltpu.CompilerParams(vmem_limit_bytes=VMEM_LIMIT),
        cost_estimate=pl.CostEstimate(flops=2**24, bytes_accessed=2**23, transcendentals=0),
        name="regroup",
    )(field)


def edge_kernel(field, low, high):
    lane = lax.broadcasted_iota(jnp.int32, (16, 128), 1)
    for z in range(2):
        for group in range(5):
            last = first = jnp.zeros((16, 128), jnp.float32)
            for t in range(min(4, 18 - group * 4)):
                at = slice((group * 4 + t) * 128, (group * 4 + t) * 128 + 128)
                here = (lane & 24) == 8 * t
                last = jnp.where(here, pltpu.roll(field[z * 4 + 3, 16:32, at].astype(jnp.float32), 100 + 8 * t, 1), last)
                first = jnp.where(here, pltpu.roll(field[z * 4, 0:16, at].astype(jnp.float32), 4 + 8 * t, 1), first)
            low[z, :, group * 128 : group * 128 + 128] = last.astype(jnp.bfloat16)
            high[z, :, group * 128 : group * 128 + 128] = first.astype(jnp.bfloat16)


def edges(field):
    return pl.pallas_call(
        edge_kernel,
        out_shape=[jax.ShapeDtypeStruct((2, 16, 640), jnp.bfloat16)] * 2,
        compiler_params=pltpu.CompilerParams(vmem_limit_bytes=VMEM_LIMIT),
        name="edges",
    )(field)


def smooth_kernel(own, other, low, high, out, own_edge, other_edge, work, spread):
    own_c, other_c = [[float(v) for v in part] for part in smooth_coefficients()]
    me = lax.axis_index("gz")
    lane = lax.broadcasted_iota(jnp.int32, (16, 128), 1)
    is_low = (lane & 7) < 4

    def spread_edges(group, tiles):
        at = pl.ds(pl.multiple_of(group * 128, 128), 128)
        for z, target in ((me, own_edge), (1 - me, other_edge)):
            both = jnp.where(is_low, low[z, :, at].astype(jnp.float32), high[z, :, at].astype(jnp.float32))
            for t in range(tiles):
                for y in range(4):
                    target[(group * 4 + t) * 4 + y] = pltpu.roll(both, 124 - 32 * y - 8 * t, 1)

    def edge_group(group, carry):
        spread_edges(group, 4)
        return carry

    lax.fori_loop(0, 4, edge_group, 0)
    spread_edges(4, 2)

    def beside(ref, y, center):
        sides = pltpu.roll(center, 1, 1) + pltpu.roll(center, 383, 1)
        return sides + (ref(y - 1) + ref(y + 1))

    def own_at(y):
        return jnp.concatenate([own[y], own_edge[y]], axis=1)

    def other_at(y):
        return jnp.concatenate([other[y], other_edge[y]], axis=1)

    def each(begin, end, unroll, body):
        def some(step, carry):
            for t in range(unroll):
                body(begin + step * unroll + t)
            return carry

        lax.fori_loop(0, (end - begin) // unroll, some, 0)

    def first(y):
        center = own_at(y)
        work[0, y] = center * own_c[2] + other_at(y) * other_c[2] + beside(own_at, y, center) * own_c[3]

    def second(y):
        center = work[0, y]
        work[1, y] = own_at(y) * own_c[1] + other_at(y) * other_c[1] + beside(lambda i: work[0, i], y, center)

    def third(y):
        center = work[1, y]
        value = beside(lambda i: work[1, i], y, center)[:, 0:256]
        value = own[y] * own_c[0] + other[y] * other_c[0] + value
        for half in range(2):
            spread[pl.ds(half * 16 * PAD + y - 4, 16, stride=PAD), :] = value[:, half * 128 : half * 128 + 128]

    each(2, 70, 34, first)
    each(3, 69, 33, second)
    each(4, 68, 32, third)
    for half in range(2):
        for k in range(16):
            out[0, k * 64 : k * 64 + 64, half * 128 : half * 128 + 128] = spread[pl.ds((half * 16 + k) * PAD, 64), :]


def smooth(own, other, low, high):
    return pl.pallas_call(
        smooth_kernel,
        out_shape=jax.ShapeDtypeStruct((1, 1024, 256), jnp.float32),
        scratch_shapes=[
            pltpu.VMEM((72, 16, 128), jnp.float32),
            pltpu.VMEM((72, 16, 128), jnp.float32),
            pltpu.VMEM((2, 72, 16, 384), jnp.float32),
            pltpu.VMEM((32 * PAD, 128), jnp.float32),
        ],
        compiler_params=pltpu.CompilerParams(vmem_limit_bytes=VMEM_LIMIT),
        name="smooth",
    )(own, other, low, high)


def ring(value, axis, steps):
    count = lax.axis_size(axis)
    return lax.ppermute(value, axis, [(i, (i + steps) % count) for i in range(count)])


def between_y(value, target):
    pairs = []
    for y_hi in range(2):
        for gz in range(2):
            to_hi, to_gz = target(y_hi, gz)
            pairs.append((y_hi * 2 + gz, to_hi * 2 + to_gz))
    return lax.ppermute(value, ("yh", "gz"), pairs)


def shards(velocity_hat):
    x_matrix, x_twist, y_matrix, y_twist = tables()
    parts = velocity_hat.reshape((3, 2) + velocity_hat.shape[3:])

    def exchanged(array, axes):
        return lax.all_to_all(array, axes, split_axis=0, concat_axis=0, tiled=True)

    def lines(fields, after=()):
        return x_transform(fields, parts, x_matrix, x_twist, after)

    curl_own, curl_other = lines(("curl_x", "curl_y"))
    curl_z = lines(("curl_z",), (curl_own,))[0]
    term_own, term_other = lines(("u", "v"), (curl_z,))
    came = between_y(curl_other, lambda y_hi, gz: (1 - y_hi, gz))
    near = between_y(term_own, lambda y_hi, gz: (y_hi, 1 - gz))
    across = between_y(term_other, lambda y_hi, gz: (1 - y_hi, 1 - gz))
    line_2 = exchanged(curl_z, ("zc", "col"))
    came_2 = between_y(line_2[:, 64:], lambda y_hi, gz: (1 - y_hi, gz))
    both = exchanged(meet(curl_own, came, near, across), ("zc", "col"))
    squares = y_transform(y_first, (line_2, came_2), y_matrix, y_twist)
    magnitude = y_transform(y_last, (both, squares), y_matrix, y_twist)
    field = exchanged(magnitude, ("gz", "col"))
    last, first = edges(field)
    low, high = ring(last, ("yh", "zc"), 1), ring(first, ("yh", "zc"), -1)
    own, other = regroup(field)
    return smooth(own, other, low, high)


def solution(mesh):
    rows, cols, planes = mesh.devices.shape
    split = jax.sharding.Mesh(mesh.devices.reshape(2, rows // 2, cols, planes), ("yh", "zc", "col", "gz"))
    return jax.shard_map(
        shards,
        mesh=split,
        in_specs=(P(None, None, "gz", ("yh", "zc", "col"), None),),
        out_specs=P("gz", "col", ("yh", "zc")),
        check_vma=False,
    )
```

```python
import math

import jax
import jax.numpy as jnp
import numpy as np
from jax import lax
from jax.experimental import pallas as pl
from jax.experimental.pallas import tpu as pltpu
from jax.sharding import PartitionSpec as P

GRID = 4096
RELAX = 0.15
VMEM_LIMIT = 28 * 1024 * 1024
PAD = 72
NT = (((1,), (1,)), ((), ()))


def cos_sin(rows, columns, period):
    turn = rows[:, None] * columns[None, :] % period
    angle = turn.astype(jnp.float32) * (2.0 * math.pi / period)
    return jnp.cos(angle), jnp.sin(angle)


def split_bf16(table):
    high = lax.reduce_precision(table, exponent_bits=8, mantissa_bits=7)
    return jnp.concatenate([high, table - high], axis=0).astype(jnp.bfloat16)


def tables():
    k, j, b = jnp.arange(128), jnp.arange(64), jnp.arange(64)
    blocks = []
    for s in range(2):
        c, d = cos_sin(b * 2 + s, k, 128)
        blocks.append(jnp.concatenate([c, -d], axis=1))
        blocks.append(jnp.concatenate([d, c], axis=1))
    x_matrix = split_bf16(jnp.concatenate(blocks, axis=0))
    x_twist = jnp.stack(cos_sin(jnp.arange(32), k, 4096)) / 64
    zero = jnp.zeros((64, 64), jnp.float32)
    c, d = cos_sin(j, j, 64)
    y_matrix = split_bf16(
        jnp.concatenate(
            [jnp.concatenate([c, zero, -d, zero], axis=1), jnp.concatenate([zero, c, zero, -d], axis=1)], axis=0
        )
    )
    y_twist = jnp.stack(cos_sin(j, j, 4096)) / 64
    return x_matrix, x_twist, y_matrix, jnp.concatenate([y_twist, y_twist], axis=2)


def turned(value, num, den):
    re, im = value
    num = num % den
    if num == 0:
        return value
    if 2 * num == den:
        return (-re, -im)
    if 4 * num == den:
        return (-im, re)
    if 4 * num == 3 * den:
        return (im, -re)
    if 8 * num == den:
        r = math.sqrt(0.5)
        return ((re - im) * r, (re + im) * r)
    if 8 * num == 3 * den:
        r = math.sqrt(0.5)
        return ((re + im) * -r, (re - im) * r)
    c, s = math.cos(2 * math.pi * num / den), math.sin(2 * math.pi * num / den)
    return (re * c - im * s, re * s + im * c)


def plus(a, b):
    return (a[0] + b[0], a[1] + b[1])


def minus(a, b):
    return (a[0] - b[0], a[1] - b[1])


def dft4(v):
    a, b = plus(v[0], v[2]), minus(v[0], v[2])
    c, d = plus(v[1], v[3]), minus(v[1], v[3])
    return [plus(a, c), (b[0] - d[1], b[1] + d[0]), minus(a, c), (b[0] + d[1], b[1] - d[0])]


def dft8(v):
    even, odd = dft4(v[0::2]), dft4(v[1::2])
    odd = [turned(odd[t], t, 8) for t in range(4)]
    return [plus(e, o) for e, o in zip(even, odd)] + [minus(e, o) for e, o in zip(even, odd)]


def x_kernel(fields, rows_local, *refs):
    n_in = 2 if fields == ("curl_z",) or fields[0] == "u" else 3
    n_out = 2 if len(fields) == 2 else 1
    ins, (matrix, twist), refs = refs[:n_in], refs[n_in : n_in + 2], refs[n_in + 2 :]
    outs, (stage, lines, spread) = refs[-3 - n_out : -3], refs[-3:]
    step = pl.program_id(0)
    scale = 2.0 * math.pi / GRID
    lane = lax.broadcasted_iota(jnp.int32, (16, 128), 1)
    row = lax.broadcasted_iota(jnp.int32, (16, 128), 0)
    start = lax.axis_index(("yh", "zc", "col")) * rows_local + step * 16
    ky = row + start
    wave_y = jnp.where(ky >= GRID // 2, ky - GRID, ky).astype(jnp.float32) * scale

    def tile(ref, part, q):
        return ref[0, part, :, pl.ds(q * 128, 128)].astype(jnp.float32)

    def wave_x(q):
        base = q * 128 - (GRID if q >= 16 else 0)
        return (lane + base).astype(jnp.float32) * scale

    def value_of(field, q):
        if field == "curl_z":
            u, v = ins
            wx = wave_x(q)
            return (
                wave_y * tile(u, 1, q) - wx * tile(v, 1, q),
                wx * tile(v, 0, q) - wave_y * tile(u, 0, q),
            )
        if field == "u":
            return (tile(ins[0], 0, q), tile(ins[0], 1, q))
        if field == "v":
            return (tile(ins[1], 0, q), tile(ins[1], 1, q))
        u, v, w = ins
        if field == "curl_x":
            return (tile(v, 0, q) - wave_y * tile(w, 1, q), tile(v, 1, q) + wave_y * tile(w, 0, q))
        wx = wave_x(q)
        return (wx * tile(w, 1, q) - tile(u, 0, q), -wx * tile(w, 0, q) - tile(u, 1, q))

    for index, field in enumerate(fields):
        for a in range(8):
            for b, value in enumerate(dft4([value_of(field, a + 8 * t) for t in range(4)])):
                value = turned(value, a * b, 32)
                stage[0, b * 8 + a] = value[0]
                stage[1, b * 8 + a] = value[1]
        for b in range(4):
            for t, value in enumerate(dft8([(stage[0, b * 8 + a], stage[1, b * 8 + a]) for a in range(8)])):
                n = b + 4 * t
                c, s = twist[0, n : n + 1, :], twist[1, n : n + 1, :]
                at = pl.ds(((n % 16) * 2 + n // 16) * 64 + step * 16, 16)
                lines[index, at, 0:128] = (value[0] * c - value[1] * s).astype(jnp.bfloat16)
                lines[index, at, 128:256] = (value[0] * s + value[1] * c).astype(jnp.bfloat16)

    @pl.when(step == 3)
    def _():
        for index in range(len(fields)):
            for pair in range(8):
                got = lax.dot_general(
                    matrix[...], lines[index, pl.ds(pair * 256, 256), :], NT, preferred_element_type=jnp.float32
                )
                got = got[0:256] + got[256:512]
                for half in range(2):
                    n16 = pair * 2 + half
                    for s in range(2):
                        for c in range(2):
                            at = (s * 2 + c) * 64
                            spread[pl.ds(c * 32 + s * 16 + n16, 64, stride=PAD), :] = got[
                                at : at + 64, half * 128 : half * 128 + 128
                            ]
            for half in range(2):
                first = (lax.axis_index("yh") + half) % 2 * (32 * PAD)
                for b in range(32):
                    at = pl.ds(pl.multiple_of(first + b * PAD, 8), 64)
                    block = spread[at, :].astype(jnp.bfloat16)
                    if n_out == 1:
                        outs[0][b, half * 64 : half * 64 + 64, :] = block
                    else:
                        outs[half][b, index * 64 : index * 64 + 64, :] = block


def x_transform(fields, parts, x_matrix, x_twist, after=()):
    rows_local = parts.shape[2]
    comps = (0, 1, 2) if fields[0] == "curl_x" else (0, 1)
    specs = [pl.BlockSpec((1, 2, 16, GRID), lambda i, comp=comp: (comp, 0, i, 0)) for comp in comps] + [
        pl.BlockSpec((512, 256), lambda i: (0, 0)),
        pl.BlockSpec((2, 32, 128), lambda i: (0, 0, 0)),
    ]
    specs += [pl.BlockSpec(memory_space=pl.ANY)] * len(after)
    return pl.pallas_call(
        lambda *refs: x_kernel(fields, rows_local, *refs),
        grid=(rows_local // 16,),
        in_specs=specs,
        out_specs=[pl.BlockSpec((32, 128, 128), lambda i: (0, 0, 0))] * len(fields),
        out_shape=[jax.ShapeDtypeStruct((32, 128, 128), jnp.bfloat16)] * len(fields),
        scratch_shapes=[
            pltpu.VMEM((2, 32, 16, 128), jnp.float32),
            pltpu.VMEM((len(fields), 2048, 256), jnp.bfloat16),
            pltpu.VMEM((65 * PAD, 128), jnp.float32),
        ],
        compiler_params=pltpu.CompilerParams(vmem_limit_bytes=VMEM_LIMIT),
        cost_estimate=pl.CostEstimate(flops=2**30, bytes_accessed=2**22, transcendentals=0),
        name="lines_" + "_".join(fields),
    )(*[parts] * len(comps), x_matrix, x_twist, *after)


def meet_kernel(own, came, near, across, out):
    for b in range(out.shape[0]):
        for index, sign in ((0, -1.0), (1, 1.0)):
            rows, term_rows = slice(index * 64, index * 64 + 64), slice(64 - index * 64, 128 - index * 64)
            for half, (field, term) in enumerate(((own, near), (came, across))):
                value = field[b, rows, :].astype(jnp.float32) + sign * term[b, term_rows, :].astype(jnp.float32)
                at = index * 128 + half * 64
                out[b, at : at + 64, :] = value.astype(jnp.bfloat16)


def meet(own, came, near, across):
    return pl.pallas_call(
        meet_kernel,
        grid=(2,),
        in_specs=[pl.BlockSpec((16, 128, 128), lambda i: (i, 0, 0))] * 4,
        out_specs=pl.BlockSpec((16, 256, 128), lambda i: (i, 0, 0)),
        out_shape=jax.ShapeDtypeStruct((32, 256, 128), jnp.bfloat16),
        compiler_params=pltpu.CompilerParams(vmem_limit_bytes=VMEM_LIMIT),
        cost_estimate=pl.CostEstimate(flops=2**20, bytes_accessed=2**22, transcendentals=0),
        name="meet",
    )(own, came, near, across)


def y_lines(sources, twist, stage, lines):
    def one(part, carry):
        def load(c, d):
            source, first = sources[d // 32]
            return source[d % 32, pl.ds(first + c * 32 + part * 16, 16), :].astype(jnp.float32)

        for a in range(8):
            values = [(load(0, a + 8 * t), load(1, a + 8 * t)) for t in range(8)]
            for b, value in enumerate(dft8(values)):
                value = turned(value, a * b, 64)
                stage[0, b * 8 + a] = value[0]
                stage[1, b * 8 + a] = value[1]
        for b in range(8):
            for t, value in enumerate(dft8([(stage[0, b * 8 + a], stage[1, b * 8 + a]) for a in range(8)])):
                n = b + 8 * t
                c, s = twist[0, n : n + 1, :], twist[1, n : n + 1, :]
                at = pl.ds(n * 32 + part * 16, 16)
                lines[at, 0:128] = (value[0] * c - value[1] * s).astype(jnp.bfloat16)
                lines[at, 128:256] = (value[0] * s + value[1] * c).astype(jnp.bfloat16)
        return carry

    lax.fori_loop(0, 2, one, 0)


def y_squares(sources, matrix, twist, stage, lines, add):
    y_lines(sources, twist, stage, lines)
    for chunk in range(8):
        got = lax.dot_general(
            matrix[...], lines[pl.ds(chunk * 256, 256), :], NT, preferred_element_type=jnp.float32
        )
        got = got[0:128] + got[128:256]
        add((slice(None), slice(chunk * 256, chunk * 256 + 256)), got * got)


def y_first(own, came, matrix, twist, out, stage, lines):
    def add(at, square):
        out[at] = 1.0 + square

    y_squares(((own, 0), (came, 0)), matrix, twist, stage, lines, add)


def y_last(source, before, matrix, twist, out, stage, lines, total):
    def add(at, square):
        total[at] = before[at] + square

    def finish(at, square):
        total[at] = jnp.sqrt(total[at] + square)

    y_squares(((source, 0), (source, 64)), matrix, twist, stage, lines, add)
    y_squares(((source, 128), (source, 192)), matrix, twist, stage, lines, finish)

    def put(h, tile, value):
        value = value.astype(jnp.bfloat16)
        for c in range(4):
            for z in range(2):
                out[z * 4 + c, h * 16 : h * 16 + 16, tile * 128 : tile * 128 + 128] = value[c * 16 : c * 16 + 16]

    for h in range(2):
        rows = slice(h * 64, h * 64 + 64)
        for tile in range(16):
            put(h, tile + 1, total[rows, tile * 128 : tile * 128 + 128])
        put(h, 0, pltpu.roll(total[rows, 15 * 128 : 16 * 128], 1, 0))
        put(h, 17, pltpu.roll(total[rows, 0:128], 63, 0))


def y_transform(kernel, sources, y_matrix, y_twist):
    last = kernel is y_last
    sums = jax.ShapeDtypeStruct((128, 2048), jnp.float32)
    scratch = [pltpu.VMEM((2, 64, 16, 128), jnp.float32), pltpu.VMEM((2048, 256), jnp.bfloat16)]
    return pl.pallas_call(
        kernel,
        out_shape=jax.ShapeDtypeStruct((8, 32, 2304), jnp.bfloat16) if last else sums,
        scratch_shapes=scratch + ([pltpu.VMEM((128, 2048), jnp.float32)] if last else []),
        compiler_params=pltpu.CompilerParams(vmem_limit_bytes=VMEM_LIMIT),
        cost_estimate=pl.CostEstimate(flops=2**28, bytes_accessed=2**22, transcendentals=0),
        name=kernel.__name__,
    )(*sources, y_matrix, y_twist)


def smooth_coefficients():
    w = RELAX
    even = np.polynomial.polynomial.polypow([1 - 6 * w + 2 * w, w], 3)
    odd = np.polynomial.polynomial.polypow([1 - 6 * w - 2 * w, w], 3)
    return (even + odd) / 2, (even - odd) / 2


def regroup_kernel(field, own, other):
    me = lax.axis_index("gz")
    lane = lax.broadcasted_iota(jnp.int32, (16, 128), 1)

    def swapped(a, b, width):
        upper = (lane & width) != 0
        return (
            jnp.where(upper, pltpu.roll(b, width, 1), a),
            jnp.where(upper, b, pltpu.roll(a, 128 - width, 1)),
        )

    def regroup(z, target, tile):
        at = pl.ds(pl.multiple_of(tile * 128, 128), 128)
        for ch in range(2):
            v = {
                (c, h): field[z * 4 + ch * 2 + c, h * 16 : h * 16 + 16, at].astype(jnp.float32)
                for c in range(2)
                for h in range(2)
            }
            p = {}
            for h in range(2):
                p[0, h], p[1, h] = swapped(v[0, h], v[1, h], 64)
            for y1 in range(2):
                s0, s1 = swapped(p[y1, 0], p[y1, 1], 16)
                y00, y01 = swapped(s0, s1, 32)
                target[tile * 4 + y1 * 2, :, ch * 128 : ch * 128 + 128] = y00
                target[tile * 4 + y1 * 2 + 1, :, ch * 128 : ch * 128 + 128] = y01

    def both(step, carry):
        for t in range(3):
            regroup(me, own, step * 3 + t)
            regroup(1 - me, other, step * 3 + t)
        return carry

    lax.fori_loop(0, 6, both, 0)


def regroup(field):
    return pl.pallas_call(
        regroup_kernel,
        out_shape=[jax.ShapeDtypeStruct((72, 16, 256), jnp.float32)] * 2,
        compiler_params=pltpu.CompilerParams(vmem_limit_bytes=VMEM_LIMIT),
        cost_estimate=pl.CostEstimate(flops=2**24, bytes_accessed=2**23, transcendentals=0),
        name="regroup",
    )(field)


def edge_kernel(field, low, high):
    lane = lax.broadcasted_iota(jnp.int32, (16, 128), 1)
    for z in range(2):
        for group in range(5):
            last = first = jnp.zeros((16, 128), jnp.float32)
            for t in range(min(4, 18 - group * 4)):
                at = slice((group * 4 + t) * 128, (group * 4 + t) * 128 + 128)
                here = (lane & 24) == 8 * t
                last = jnp.where(here, pltpu.roll(field[z * 4 + 3, 16:32, at].astype(jnp.float32), 100 + 8 * t, 1), last)
                first = jnp.where(here, pltpu.roll(field[z * 4, 0:16, at].astype(jnp.float32), 4 + 8 * t, 1), first)
            low[z, :, group * 128 : group * 128 + 128] = last.astype(jnp.bfloat16)
            high[z, :, group * 128 : group * 128 + 128] = first.astype(jnp.bfloat16)


def edges(field):
    return pl.pallas_call(
        edge_kernel,
        out_shape=[jax.ShapeDtypeStruct((2, 16, 640), jnp.bfloat16)] * 2,
        compiler_params=pltpu.CompilerParams(vmem_limit_bytes=VMEM_LIMIT),
        name="edges",
    )(field)


def smooth_kernel(own, other, low, high, out, own_edge, other_edge, work, spread):
    own_c, other_c = [[float(v) for v in part] for part in smooth_coefficients()]
    me = lax.axis_index("gz")
    lane = lax.broadcasted_iota(jnp.int32, (16, 128), 1)
    is_low = (lane & 7) < 4

    def spread_edges(group, tiles):
        at = pl.ds(pl.multiple_of(group * 128, 128), 128)
        for z, target in ((me, own_edge), (1 - me, other_edge)):
            both = jnp.where(is_low, low[z, :, at].astype(jnp.float32), high[z, :, at].astype(jnp.float32))
            for t in range(tiles):
                for y in range(4):
                    target[(group * 4 + t) * 4 + y] = pltpu.roll(both, 124 - 32 * y - 8 * t, 1)

    def edge_group(group, carry):
        spread_edges(group, 4)
        return carry

    lax.fori_loop(0, 4, edge_group, 0)
    spread_edges(4, 2)

    def beside(ref, y, center):
        sides = pltpu.roll(center, 1, 1) + pltpu.roll(center, 383, 1)
        return sides + (ref(y - 1) + ref(y + 1))

    def own_at(y):
        return jnp.concatenate([own[y], own_edge[y]], axis=1)

    def other_at(y):
        return jnp.concatenate([other[y], other_edge[y]], axis=1)

    def each(begin, end, unroll, body):
        def some(step, carry):
            for t in range(unroll):
                body(begin + step * unroll + t)
            return carry

        lax.fori_loop(0, (end - begin) // unroll, some, 0)

    def first(y):
        center = own_at(y)
        work[0, y] = center * own_c[2] + other_at(y) * other_c[2] + beside(own_at, y, center) * own_c[3]

    def second(y):
        center = work[0, y]
        work[1, y] = own_at(y) * own_c[1] + other_at(y) * other_c[1] + beside(lambda i: work[0, i], y, center)

    def third(y):
        center = work[1, y]
        value = beside(lambda i: work[1, i], y, center)[:, 0:256]
        value = own[y] * own_c[0] + other[y] * other_c[0] + value
        for half in range(2):
            spread[pl.ds(half * 16 * PAD + y - 4, 16, stride=PAD), :] = value[:, half * 128 : half * 128 + 128]

    each(2, 70, 34, first)
    each(3, 69, 33, second)
    each(4, 68, 32, third)
    for half in range(2):
        for k in range(16):
            out[0, k * 64 : k * 64 + 64, half * 128 : half * 128 + 128] = spread[pl.ds((half * 16 + k) * PAD, 64), :]


def smooth(own, other, low, high):
    return pl.pallas_call(
        smooth_kernel,
        out_shape=jax.ShapeDtypeStruct((1, 1024, 256), jnp.float32),
        scratch_shapes=[
            pltpu.VMEM((72, 16, 128), jnp.float32),
            pltpu.VMEM((72, 16, 128), jnp.float32),
            pltpu.VMEM((2, 72, 16, 384), jnp.float32),
            pltpu.VMEM((33 * PAD, 128), jnp.float32),
        ],
        compiler_params=pltpu.CompilerParams(vmem_limit_bytes=VMEM_LIMIT),
        name="smooth",
    )(own, other, low, high)


def ring(value, axis, steps):
    count = lax.axis_size(axis)
    return lax.ppermute(value, axis, [(i, (i + steps) % count) for i in range(count)])


def between_y(value, target):
    pairs = []
    for y_hi in range(2):
        for gz in range(2):
            to_hi, to_gz = target(y_hi, gz)
            pairs.append((y_hi * 2 + gz, to_hi * 2 + to_gz))
    return lax.ppermute(value, ("yh", "gz"), pairs)


def shards(velocity_hat):
    x_matrix, x_twist, y_matrix, y_twist = tables()
    parts = velocity_hat.reshape((3, 2) + velocity_hat.shape[3:])

    def exchanged(array, axes):
        return lax.all_to_all(array, axes, split_axis=0, concat_axis=0, tiled=True)

    def lines(fields, after=()):
        return x_transform(fields, parts, x_matrix, x_twist, after)

    curl_own, curl_other = lines(("curl_x", "curl_y"))
    curl_z = lines(("curl_z",), (curl_own,))[0]
    term_own, term_other = lines(("u", "v"), (curl_z,))
    came = between_y(curl_other, lambda y_hi, gz: (1 - y_hi, gz))
    near = between_y(term_own, lambda y_hi, gz: (y_hi, 1 - gz))
    across = between_y(term_other, lambda y_hi, gz: (1 - y_hi, 1 - gz))
    line_2 = exchanged(curl_z, ("zc", "col"))
    came_2 = between_y(line_2[:, 64:], lambda y_hi, gz: (1 - y_hi, gz))
    both = exchanged(meet(curl_own, came, near, across), ("zc", "col"))
    squares = y_transform(y_first, (line_2, came_2), y_matrix, y_twist)
    magnitude = y_transform(y_last, (both, squares), y_matrix, y_twist)
    field = exchanged(magnitude, ("gz", "col"))
    last, first = edges(field)
    low, high = ring(last, ("yh", "zc"), 1), ring(first, ("yh", "zc"), -1)
    own, other = regroup(field)
    return smooth(own, other, low, high)


def solution(mesh):
    rows, cols, planes = mesh.devices.shape
    split = jax.sharding.Mesh(mesh.devices.reshape(2, rows // 2, cols, planes), ("yh", "zc", "col", "gz"))
    return jax.shard_map(
        shards,
        mesh=split,
        in_specs=(P(None, None, "gz", ("yh", "zc", "col"), None),),
        out_specs=P("gz", "col", ("yh", "zc")),
        check_vma=False,
    )
```

```python
import math

import jax
import jax.numpy as jnp
import numpy as np
from jax import lax
from jax.experimental import pallas as pl
from jax.experimental.pallas import tpu as pltpu
from jax.sharding import PartitionSpec as P

GRID = 4096
RELAX = 0.15
VMEM_LIMIT = 28 * 1024 * 1024
PAD = 72
NT = (((1,), (1,)), ((), ()))


def cos_sin(rows, columns, period):
    turn = rows[:, None] * columns[None, :] % period
    angle = turn.astype(jnp.float32) * (2.0 * math.pi / period)
    return jnp.cos(angle), jnp.sin(angle)


def split_bf16(table):
    high = lax.reduce_precision(table, exponent_bits=8, mantissa_bits=7)
    return jnp.concatenate([high, table - high], axis=0).astype(jnp.bfloat16)


def tables():
    k, j, b = jnp.arange(128), jnp.arange(64), jnp.arange(64)
    blocks = []
    for s in range(2):
        c, d = cos_sin(b * 2 + s, k, 128)
        blocks.append(jnp.concatenate([c, -d], axis=1))
        blocks.append(jnp.concatenate([d, c], axis=1))
    x_matrix = split_bf16(jnp.concatenate(blocks, axis=0))
    x_twist = jnp.stack(cos_sin(jnp.arange(32), k, 4096)) / 64
    zero = jnp.zeros((64, 64), jnp.float32)
    c, d = cos_sin(j, j, 64)
    y_matrix = split_bf16(
        jnp.concatenate(
            [jnp.concatenate([c, zero, -d, zero], axis=1), jnp.concatenate([zero, c, zero, -d], axis=1)], axis=0
        )
    )
    y_twist = jnp.stack(cos_sin(j, j, 4096)) / 64
    return x_matrix, x_twist, y_matrix, jnp.concatenate([y_twist, y_twist], axis=2)


def turned(value, num, den):
    re, im = value
    num = num % den
    if num == 0:
        return value
    if 2 * num == den:
        return (-re, -im)
    if 4 * num == den:
        return (-im, re)
    if 4 * num == 3 * den:
        return (im, -re)
    if 8 * num == den:
        r = math.sqrt(0.5)
        return ((re - im) * r, (re + im) * r)
    if 8 * num == 3 * den:
        r = math.sqrt(0.5)
        return ((re + im) * -r, (re - im) * r)
    c, s = math.cos(2 * math.pi * num / den), math.sin(2 * math.pi * num / den)
    return (re * c - im * s, re * s + im * c)


def plus(a, b):
    return (a[0] + b[0], a[1] + b[1])


def minus(a, b):
    return (a[0] - b[0], a[1] - b[1])


def dft4(v):
    a, b = plus(v[0], v[2]), minus(v[0], v[2])
    c, d = plus(v[1], v[3]), minus(v[1], v[3])
    return [plus(a, c), (b[0] - d[1], b[1] + d[0]), minus(a, c), (b[0] + d[1], b[1] - d[0])]


def dft8(v):
    even, odd = dft4(v[0::2]), dft4(v[1::2])
    odd = [turned(odd[t], t, 8) for t in range(4)]
    return [plus(e, o) for e, o in zip(even, odd)] + [minus(e, o) for e, o in zip(even, odd)]


def x_kernel(fields, rows_local, *refs):
    n_in = 2 if fields == ("curl_z",) or fields[0] == "u" else 3
    n_out = 2 if len(fields) == 2 else 1
    ins, (matrix, twist), refs = refs[:n_in], refs[n_in : n_in + 2], refs[n_in + 2 :]
    outs, (stage, lines, spread) = refs[-3 - n_out : -3], refs[-3:]
    step = pl.program_id(0)
    scale = 2.0 * math.pi / GRID
    lane = lax.broadcasted_iota(jnp.int32, (16, 128), 1)
    row = lax.broadcasted_iota(jnp.int32, (16, 128), 0)
    start = lax.axis_index(("yh", "zc", "col")) * rows_local + step * 16
    ky = row + start
    wave_y = jnp.where(ky >= GRID // 2, ky - GRID, ky).astype(jnp.float32) * scale

    def tile(ref, part, q):
        return ref[0, part, :, pl.ds(q * 128, 128)].astype(jnp.float32)

    def wave_x(q):
        base = q * 128 - (GRID if q >= 16 else 0)
        return (lane + base).astype(jnp.float32) * scale

    def value_of(field, q):
        if field == "curl_z":
            u, v = ins
            wx = wave_x(q)
            return (
                wave_y * tile(u, 1, q) - wx * tile(v, 1, q),
                wx * tile(v, 0, q) - wave_y * tile(u, 0, q),
            )
        if field == "u":
            return (tile(ins[0], 0, q), tile(ins[0], 1, q))
        if field == "v":
            return (tile(ins[1], 0, q), tile(ins[1], 1, q))
        u, v, w = ins
        if field == "curl_x":
            return (tile(v, 0, q) - wave_y * tile(w, 1, q), tile(v, 1, q) + wave_y * tile(w, 0, q))
        wx = wave_x(q)
        return (wx * tile(w, 1, q) - tile(u, 0, q), -wx * tile(w, 0, q) - tile(u, 1, q))

    for index, field in enumerate(fields):
        for a in range(8):
            for b, value in enumerate(dft4([value_of(field, a + 8 * t) for t in range(4)])):
                value = turned(value, a * b, 32)
                stage[0, b * 8 + a] = value[0]
                stage[1, b * 8 + a] = value[1]
        for b in range(4):
            for t, value in enumerate(dft8([(stage[0, b * 8 + a], stage[1, b * 8 + a]) for a in range(8)])):
                n = b + 4 * t
                c, s = twist[0, n : n + 1, :], twist[1, n : n + 1, :]
                at = pl.ds(((n % 16) * 2 + n // 16) * 64 + step * 16, 16)
                lines[index, at, 0:128] = (value[0] * c - value[1] * s).astype(jnp.bfloat16)
                lines[index, at, 128:256] = (value[0] * s + value[1] * c).astype(jnp.bfloat16)

    @pl.when(step == 3)
    def _():
        for index in range(len(fields)):
            for pair in range(8):
                got = lax.dot_general(
                    matrix[...], lines[index, pl.ds(pair * 256, 256), :], NT, preferred_element_type=jnp.float32
                )
                got = got[0:256] + got[256:512]
                for half in range(2):
                    n16 = pair * 2 + half
                    for s in range(2):
                        for c in range(2):
                            at = (s * 2 + c) * 64
                            spread[pl.ds(c * 32 + s * 16 + n16, 64, stride=PAD), :] = got[
                                at : at + 64, half * 128 : half * 128 + 128
                            ]
            for half in range(2):
                first = (lax.axis_index("yh") + half) % 2 * (32 * PAD)
                for b in range(32):
                    at = pl.ds(pl.multiple_of(first + b * PAD, 8), 64)
                    block = spread[at, :].astype(jnp.bfloat16)
                    if n_out == 1:
                        outs[0][b, half * 64 : half * 64 + 64, :] = block
                    else:
                        outs[half][b, index * 64 : index * 64 + 64, :] = block


def x_transform(fields, parts, x_matrix, x_twist, after=()):
    rows_local = parts.shape[2]
    comps = (0, 1, 2) if fields[0] == "curl_x" else (0, 1)
    specs = [pl.BlockSpec((1, 2, 16, GRID), lambda i, comp=comp: (comp, 0, i, 0)) for comp in comps] + [
        pl.BlockSpec((512, 256), lambda i: (0, 0)),
        pl.BlockSpec((2, 32, 128), lambda i: (0, 0, 0)),
    ]
    specs += [pl.BlockSpec(memory_space=pl.ANY)] * len(after)
    return pl.pallas_call(
        lambda *refs: x_kernel(fields, rows_local, *refs),
        grid=(rows_local // 16,),
        in_specs=specs,
        out_specs=[pl.BlockSpec((32, 128, 128), lambda i: (0, 0, 0))] * len(fields),
        out_shape=[jax.ShapeDtypeStruct((32, 128, 128), jnp.bfloat16)] * len(fields),
        scratch_shapes=[
            pltpu.VMEM((2, 32, 16, 128), jnp.float32),
            pltpu.VMEM((len(fields), 2048, 256), jnp.bfloat16),
            pltpu.VMEM((65 * PAD, 128), jnp.float32),
        ],
        compiler_params=pltpu.CompilerParams(vmem_limit_bytes=VMEM_LIMIT),
        cost_estimate=pl.CostEstimate(flops=2**30, bytes_accessed=2**22, transcendentals=0),
        name="lines_" + "_".join(fields),
    )(*[parts] * len(comps), x_matrix, x_twist, *after)


def meet_kernel(own, came, near, across, out):
    for b in range(out.shape[0]):
        for index, sign in ((0, -1.0), (1, 1.0)):
            rows, term_rows = slice(index * 64, index * 64 + 64), slice(64 - index * 64, 128 - index * 64)
            for half, (field, term) in enumerate(((own, near), (came, across))):
                value = field[b, rows, :].astype(jnp.float32) + sign * term[b, term_rows, :].astype(jnp.float32)
                at = index * 128 + half * 64
                out[b, at : at + 64, :] = value.astype(jnp.bfloat16)


def meet(own, came, near, across):
    return pl.pallas_call(
        meet_kernel,
        grid=(2,),
        in_specs=[pl.BlockSpec((16, 128, 128), lambda i: (i, 0, 0))] * 4,
        out_specs=pl.BlockSpec((16, 256, 128), lambda i: (i, 0, 0)),
        out_shape=jax.ShapeDtypeStruct((32, 256, 128), jnp.bfloat16),
        compiler_params=pltpu.CompilerParams(vmem_limit_bytes=VMEM_LIMIT),
        cost_estimate=pl.CostEstimate(flops=2**20, bytes_accessed=2**22, transcendentals=0),
        name="meet",
    )(own, came, near, across)


def y_lines(sources, twist, stage, lines):
    def one(part, carry):
        def load(c, d):
            source, first = sources[d // 32]
            return source[d % 32, pl.ds(first + c * 32 + part * 16, 16), :].astype(jnp.float32)

        for a in range(8):
            values = [(load(0, a + 8 * t), load(1, a + 8 * t)) for t in range(8)]
            for b, value in enumerate(dft8(values)):
                value = turned(value, a * b, 64)
                stage[0, b * 8 + a] = value[0]
                stage[1, b * 8 + a] = value[1]
        for b in range(8):
            for t, value in enumerate(dft8([(stage[0, b * 8 + a], stage[1, b * 8 + a]) for a in range(8)])):
                n = b + 8 * t
                c, s = twist[0, n : n + 1, :], twist[1, n : n + 1, :]
                at = pl.ds(n * 32 + part * 16, 16)
                lines[at, 0:128] = (value[0] * c - value[1] * s).astype(jnp.bfloat16)
                lines[at, 128:256] = (value[0] * s + value[1] * c).astype(jnp.bfloat16)
        return carry

    lax.fori_loop(0, 2, one, 0)


def y_squares(sources, matrix, twist, stage, lines, add):
    y_lines(sources, twist, stage, lines)
    for chunk in range(8):
        got = lax.dot_general(
            matrix[...], lines[pl.ds(chunk * 256, 256), :], NT, preferred_element_type=jnp.float32
        )
        got = got[0:128] + got[128:256]
        add((slice(None), slice(chunk * 256, chunk * 256 + 256)), got * got)


def y_first(own, came, matrix, twist, out, stage, lines):
    def add(at, square):
        out[at] = 1.0 + square

    y_squares(((own, 0), (came, 0)), matrix, twist, stage, lines, add)


def y_last(source, before, matrix, twist, out, stage, lines, total):
    def add(at, square):
        total[at] = before[at] + square

    def finish(at, square):
        total[at] = jnp.sqrt(total[at] + square)

    y_squares(((source, 0), (source, 64)), matrix, twist, stage, lines, add)
    y_squares(((source, 128), (source, 192)), matrix, twist, stage, lines, finish)

    def put(h, tile, value):
        value = value.astype(jnp.bfloat16)
        for c in range(4):
            for z in range(2):
                out[z * 4 + c, h * 16 : h * 16 + 16, tile * 128 : tile * 128 + 128] = value[c * 16 : c * 16 + 16]

    upper = (lax.broadcasted_iota(jnp.int32, (64, 128), 0) & 15) < 8
    for h in range(2):
        rows = slice(h * 64, h * 64 + 64)
        for tile in range(16):
            put(h, tile, total[rows, tile * 128 : tile * 128 + 128])
        before_first = pltpu.roll(total[rows, 15 * 128 : 16 * 128], 1, 0)
        after_last = pltpu.roll(total[rows, 0:128], 63, 0)
        put(h, 16, jnp.where(upper, before_first, after_last))


def y_transform(kernel, sources, y_matrix, y_twist):
    last = kernel is y_last
    sums = jax.ShapeDtypeStruct((128, 2048), jnp.float32)
    scratch = [pltpu.VMEM((2, 64, 16, 128), jnp.float32), pltpu.VMEM((2048, 256), jnp.bfloat16)]
    return pl.pallas_call(
        kernel,
        out_shape=jax.ShapeDtypeStruct((8, 32, 2176), jnp.bfloat16) if last else sums,
        scratch_shapes=scratch + ([pltpu.VMEM((128, 2048), jnp.float32)] if last else []),
        compiler_params=pltpu.CompilerParams(vmem_limit_bytes=VMEM_LIMIT),
        cost_estimate=pl.CostEstimate(flops=2**28, bytes_accessed=2**22, transcendentals=0),
        name=kernel.__name__,
    )(*sources, y_matrix, y_twist)


def smooth_coefficients():
    w = RELAX
    even = np.polynomial.polynomial.polypow([1 - 6 * w + 2 * w, w], 3)
    odd = np.polynomial.polynomial.polypow([1 - 6 * w - 2 * w, w], 3)
    return (even + odd) / 2, (even - odd) / 2


def brick_tile(field, source, h, tile):
    def held(index):
        start = index * 128 if isinstance(index, int) else pl.multiple_of(index * 128, 128)
        return field[source, h * 16 : h * 16 + 16, pl.ds(start, 128)].astype(jnp.float32)

    row = lax.broadcasted_iota(jnp.int32, (16, 128), 0)
    if isinstance(tile, int) and tile == 0:
        return jnp.where(row == 0, held(16), pltpu.roll(held(15), 1, 0))
    if isinstance(tile, int) and tile == 17:
        return jnp.where(row == 15, held(16), pltpu.roll(held(0), 15, 0))
    return held(tile - 1)


def regroup_kernel(field, own, other):
    me = lax.axis_index("gz")
    lane = lax.broadcasted_iota(jnp.int32, (16, 128), 1)

    def swapped(a, b, width):
        upper = (lane & width) != 0
        return (
            jnp.where(upper, pltpu.roll(b, width, 1), a),
            jnp.where(upper, b, pltpu.roll(a, 128 - width, 1)),
        )

    def regroup(z, target, tile):
        for ch in range(2):
            v = {
                (c, h): brick_tile(field, z * 4 + ch * 2 + c, h, tile)
                for c in range(2)
                for h in range(2)
            }
            p = {}
            for h in range(2):
                p[0, h], p[1, h] = swapped(v[0, h], v[1, h], 64)
            for y1 in range(2):
                s0, s1 = swapped(p[y1, 0], p[y1, 1], 16)
                y00, y01 = swapped(s0, s1, 32)
                target[tile * 4 + y1 * 2, :, ch * 128 : ch * 128 + 128] = y00
                target[tile * 4 + y1 * 2 + 1, :, ch * 128 : ch * 128 + 128] = y01

    def both(step, carry):
        for t in range(2):
            regroup(me, own, step * 2 + t + 1)
            regroup(1 - me, other, step * 2 + t + 1)
        return carry

    lax.fori_loop(0, 8, both, 0)
    for tile in (0, 17):
        regroup(me, own, tile)
        regroup(1 - me, other, tile)


def regroup(field):
    return pl.pallas_call(
        regroup_kernel,
        out_shape=[jax.ShapeDtypeStruct((72, 16, 256), jnp.float32)] * 2,
        compiler_params=pltpu.CompilerParams(vmem_limit_bytes=VMEM_LIMIT),
        cost_estimate=pl.CostEstimate(flops=2**24, bytes_accessed=2**23, transcendentals=0),
        name="regroup",
    )(field)


def edge_kernel(field, low, high):
    lane = lax.broadcasted_iota(jnp.int32, (16, 128), 1)
    for z in range(2):
        for group in range(5):
            last = first = jnp.zeros((16, 128), jnp.float32)
            for t in range(min(4, 18 - group * 4)):
                tile = group * 4 + t
                here = (lane & 24) == 8 * t
                last = jnp.where(here, pltpu.roll(brick_tile(field, z * 4 + 3, 1, tile), 100 + 8 * t, 1), last)
                first = jnp.where(here, pltpu.roll(brick_tile(field, z * 4, 0, tile), 4 + 8 * t, 1), first)
            low[z, :, group * 128 : group * 128 + 128] = last.astype(jnp.bfloat16)
            high[z, :, group * 128 : group * 128 + 128] = first.astype(jnp.bfloat16)


def edges(field):
    return pl.pallas_call(
        edge_kernel,
        out_shape=[jax.ShapeDtypeStruct((2, 16, 640), jnp.bfloat16)] * 2,
        compiler_params=pltpu.CompilerParams(vmem_limit_bytes=VMEM_LIMIT),
        name="edges",
    )(field)


def smooth_kernel(own, other, low, high, out, own_edge, other_edge, work, spread):
    own_c, other_c = [[float(v) for v in part] for part in smooth_coefficients()]
    me = lax.axis_index("gz")
    lane = lax.broadcasted_iota(jnp.int32, (16, 128), 1)
    is_low = (lane & 7) < 4

    def spread_edges(group, tiles):
        at = pl.ds(pl.multiple_of(group * 128, 128), 128)
        for z, target in ((me, own_edge), (1 - me, other_edge)):
            both = jnp.where(is_low, low[z, :, at].astype(jnp.float32), high[z, :, at].astype(jnp.float32))
            for t in range(tiles):
                for y in range(4):
                    target[(group * 4 + t) * 4 + y] = pltpu.roll(both, 124 - 32 * y - 8 * t, 1)

    def edge_group(group, carry):
        spread_edges(group, 4)
        return carry

    lax.fori_loop(0, 4, edge_group, 0)
    spread_edges(4, 2)

    def beside(ref, y, center):
        sides = pltpu.roll(center, 1, 1) + pltpu.roll(center, 383, 1)
        return sides + (ref(y - 1) + ref(y + 1))

    def own_at(y):
        return jnp.concatenate([own[y], own_edge[y]], axis=1)

    def other_at(y):
        return jnp.concatenate([other[y], other_edge[y]], axis=1)

    def each(begin, end, unroll, body):
        def some(step, carry):
            for t in range(unroll):
                body(begin + step * unroll + t)
            return carry

        lax.fori_loop(0, (end - begin) // unroll, some, 0)

    def first(y):
        center = own_at(y)
        work[0, y] = center * own_c[2] + other_at(y) * other_c[2] + beside(own_at, y, center) * own_c[3]

    def second(y):
        center = work[0, y]
        work[1, y] = own_at(y) * own_c[1] + other_at(y) * other_c[1] + beside(lambda i: work[0, i], y, center)

    def third(y):
        center = work[1, y]
        value = beside(lambda i: work[1, i], y, center)[:, 0:256]
        value = own[y] * own_c[0] + other[y] * other_c[0] + value
        for half in range(2):
            spread[pl.ds(half * 16 * PAD + y - 4, 16, stride=PAD), :] = value[:, half * 128 : half * 128 + 128]

    each(2, 70, 34, first)
    each(3, 69, 33, second)
    each(4, 68, 32, third)
    for half in range(2):
        for k in range(16):
            out[0, k * 64 : k * 64 + 64, half * 128 : half * 128 + 128] = spread[pl.ds((half * 16 + k) * PAD, 64), :]


def smooth(own, other, low, high):
    return pl.pallas_call(
        smooth_kernel,
        out_shape=jax.ShapeDtypeStruct((1, 1024, 256), jnp.float32),
        scratch_shapes=[
            pltpu.VMEM((72, 16, 128), jnp.float32),
            pltpu.VMEM((72, 16, 128), jnp.float32),
            pltpu.VMEM((2, 72, 16, 384), jnp.float32),
            pltpu.VMEM((33 * PAD, 128), jnp.float32),
        ],
        compiler_params=pltpu.CompilerParams(vmem_limit_bytes=VMEM_LIMIT),
        name="smooth",
    )(own, other, low, high)


def ring(value, axis, steps):
    count = lax.axis_size(axis)
    return lax.ppermute(value, axis, [(i, (i + steps) % count) for i in range(count)])


def between_y(value, target):
    pairs = []
    for y_hi in range(2):
        for gz in range(2):
            to_hi, to_gz = target(y_hi, gz)
            pairs.append((y_hi * 2 + gz, to_hi * 2 + to_gz))
    return lax.ppermute(value, ("yh", "gz"), pairs)


def shards(velocity_hat):
    x_matrix, x_twist, y_matrix, y_twist = tables()
    parts = velocity_hat.reshape((3, 2) + velocity_hat.shape[3:])

    def exchanged(array, axes):
        return lax.all_to_all(array, axes, split_axis=0, concat_axis=0, tiled=True)

    def lines(fields, after=()):
        return x_transform(fields, parts, x_matrix, x_twist, after)

    curl_own, curl_other = lines(("curl_x", "curl_y"))
    curl_z = lines(("curl_z",), (curl_own,))[0]
    term_own, term_other = lines(("u", "v"), (curl_z,))
    came = between_y(curl_other, lambda y_hi, gz: (1 - y_hi, gz))
    near = between_y(term_own, lambda y_hi, gz: (y_hi, 1 - gz))
    across = between_y(term_other, lambda y_hi, gz: (1 - y_hi, 1 - gz))
    line_2 = exchanged(curl_z, ("zc", "col"))
    came_2 = between_y(line_2[:, 64:], lambda y_hi, gz: (1 - y_hi, gz))
    both = exchanged(meet(curl_own, came, near, across), ("zc", "col"))
    squares = y_transform(y_first, (line_2, came_2), y_matrix, y_twist)
    magnitude = y_transform(y_last, (both, squares), y_matrix, y_twist)
    field = exchanged(magnitude, ("gz", "col"))
    last, first = edges(field)
    low, high = ring(last, ("yh", "zc"), 1), ring(first, ("yh", "zc"), -1)
    own, other = regroup(field)
    return smooth(own, other, low, high)


def solution(mesh):
    rows, cols, planes = mesh.devices.shape
    split = jax.sharding.Mesh(mesh.devices.reshape(2, rows // 2, cols, planes), ("yh", "zc", "col", "gz"))
    return jax.shard_map(
        shards,
        mesh=split,
        in_specs=(P(None, None, "gz", ("yh", "zc", "col"), None),),
        out_specs=P("gz", "col", ("yh", "zc")),
        check_vma=False,
    )
```

```python
import math

import jax
import jax.numpy as jnp
import numpy as np
from jax import lax
from jax.experimental import pallas as pl
from jax.experimental.pallas import tpu as pltpu
from jax.sharding import PartitionSpec as P

GRID = 4096
RELAX = 0.15
VMEM_LIMIT = 40 * 1024 * 1024
PAD = 72
NT = (((1,), (1,)), ((), ()))


def cos_sin(rows, columns, period):
    turn = rows[:, None] * columns[None, :] % period
    angle = turn.astype(jnp.float32) * (2.0 * math.pi / period)
    return jnp.cos(angle), jnp.sin(angle)


def split_bf16(table):
    high = lax.reduce_precision(table, exponent_bits=8, mantissa_bits=7)
    return jnp.concatenate([high, table - high], axis=0).astype(jnp.bfloat16)


def tables():
    k, j, b = jnp.arange(128), jnp.arange(64), jnp.arange(64)
    blocks = []
    for s in range(2):
        c, d = cos_sin(b * 2 + s, k, 128)
        blocks.append(jnp.concatenate([c, -d], axis=1))
        blocks.append(jnp.concatenate([d, c], axis=1))
    x_matrix = split_bf16(jnp.concatenate(blocks, axis=0))
    x_twist = jnp.stack(cos_sin(jnp.arange(32), k, 4096)) / 64
    zero = jnp.zeros((64, 64), jnp.float32)
    c, d = cos_sin(j, j, 64)
    y_matrix = split_bf16(
        jnp.concatenate(
            [jnp.concatenate([c, zero, -d, zero], axis=1), jnp.concatenate([zero, c, zero, -d], axis=1)], axis=0
        )
    )
    y_twist = jnp.stack(cos_sin(j, j, 4096)) / 64
    return x_matrix, x_twist, y_matrix, jnp.concatenate([y_twist, y_twist], axis=2)


def turned(value, num, den):
    re, im = value
    num = num % den
    if num == 0:
        return value
    if 2 * num == den:
        return (-re, -im)
    if 4 * num == den:
        return (-im, re)
    if 4 * num == 3 * den:
        return (im, -re)
    if 8 * num == den:
        r = math.sqrt(0.5)
        return ((re - im) * r, (re + im) * r)
    if 8 * num == 3 * den:
        r = math.sqrt(0.5)
        return ((re + im) * -r, (re - im) * r)
    c, s = math.cos(2 * math.pi * num / den), math.sin(2 * math.pi * num / den)
    return (re * c - im * s, re * s + im * c)


def plus(a, b):
    return (a[0] + b[0], a[1] + b[1])


def minus(a, b):
    return (a[0] - b[0], a[1] - b[1])


def dft4(v):
    a, b = plus(v[0], v[2]), minus(v[0], v[2])
    c, d = plus(v[1], v[3]), minus(v[1], v[3])
    return [plus(a, c), (b[0] - d[1], b[1] + d[0]), minus(a, c), (b[0] + d[1], b[1] - d[0])]


def dft8(v):
    even, odd = dft4(v[0::2]), dft4(v[1::2])
    odd = [turned(odd[t], t, 8) for t in range(4)]
    return [plus(e, o) for e, o in zip(even, odd)] + [minus(e, o) for e, o in zip(even, odd)]


def x_kernel(fields, rows_local, *refs):
    n_in = 2 if fields == ("curl_z",) or fields[0] == "u" else 3
    n_out = 2 if len(fields) == 2 else 1
    ins, (matrix, twist), refs = refs[:n_in], refs[n_in : n_in + 2], refs[n_in + 2 :]
    outs, (stage, lines, spread) = refs[-3 - n_out : -3], refs[-3:]
    step = pl.program_id(0)
    scale = 2.0 * math.pi / GRID
    lane = lax.broadcasted_iota(jnp.int32, (16, 128), 1)
    row = lax.broadcasted_iota(jnp.int32, (16, 128), 0)
    start = lax.axis_index(("yh", "zc", "col")) * rows_local + step * 16
    ky = row + start
    wave_y = jnp.where(ky >= GRID // 2, ky - GRID, ky).astype(jnp.float32) * scale

    def tile(ref, part, q):
        return ref[0, part, :, pl.ds(q * 128, 128)].astype(jnp.float32)

    def wave_x(q):
        base = q * 128 - (GRID if q >= 16 else 0)
        return (lane + base).astype(jnp.float32) * scale

    def value_of(field, q):
        if field == "curl_z":
            u, v = ins
            wx = wave_x(q)
            return (
                wave_y * tile(u, 1, q) - wx * tile(v, 1, q),
                wx * tile(v, 0, q) - wave_y * tile(u, 0, q),
            )
        if field == "u":
            return (tile(ins[0], 0, q), tile(ins[0], 1, q))
        if field == "v":
            return (tile(ins[1], 0, q), tile(ins[1], 1, q))
        u, v, w = ins
        if field == "curl_x":
            return (tile(v, 0, q) - wave_y * tile(w, 1, q), tile(v, 1, q) + wave_y * tile(w, 0, q))
        wx = wave_x(q)
        return (wx * tile(w, 1, q) - tile(u, 0, q), -wx * tile(w, 0, q) - tile(u, 1, q))

    for index, field in enumerate(fields):
        for a in range(8):
            for b, value in enumerate(dft4([value_of(field, a + 8 * t) for t in range(4)])):
                value = turned(value, a * b, 32)
                stage[0, b * 8 + a] = value[0]
                stage[1, b * 8 + a] = value[1]
        for b in range(4):
            for t, value in enumerate(dft8([(stage[0, b * 8 + a], stage[1, b * 8 + a]) for a in range(8)])):
                n = b + 4 * t
                c, s = twist[0, n : n + 1, :], twist[1, n : n + 1, :]
                at = pl.ds(((n % 16) * 2 + n // 16) * 64 + step * 16, 16)
                lines[index, at, 0:128] = (value[0] * c - value[1] * s).astype(jnp.bfloat16)
                lines[index, at, 128:256] = (value[0] * s + value[1] * c).astype(jnp.bfloat16)

    @pl.when(step == 3)
    def _():
        for index in range(len(fields)):
            for pair in range(8):
                got = lax.dot_general(
                    matrix[...], lines[index, pl.ds(pair * 256, 256), :], NT, preferred_element_type=jnp.float32
                )
                got = got[0:256] + got[256:512]
                for half in range(2):
                    n16 = pair * 2 + half
                    for s in range(2):
                        for c in range(2):
                            at = (s * 2 + c) * 64
                            spread[pl.ds(c * 32 + s * 16 + n16, 64, stride=PAD), :] = got[
                                at : at + 64, half * 128 : half * 128 + 128
                            ]
            for half in range(2):
                first = (lax.axis_index("yh") + half) % 2 * (32 * PAD)
                for b in range(32):
                    at = pl.ds(pl.multiple_of(first + b * PAD, 8), 64)
                    block = spread[at, :].astype(jnp.bfloat16)
                    if n_out == 1:
                        outs[0][b, half * 64 : half * 64 + 64, :] = block
                    else:
                        outs[half][b, index * 64 : index * 64 + 64, :] = block


def x_transform(fields, parts, x_matrix, x_twist, after=()):
    rows_local = parts.shape[2]
    comps = (0, 1, 2) if fields[0] == "curl_x" else (0, 1)
    specs = [pl.BlockSpec((1, 2, 16, GRID), lambda i, comp=comp: (comp, 0, i, 0)) for comp in comps] + [
        pl.BlockSpec((512, 256), lambda i: (0, 0)),
        pl.BlockSpec((2, 32, 128), lambda i: (0, 0, 0)),
    ]
    specs += [pl.BlockSpec(memory_space=pl.ANY)] * len(after)
    return pl.pallas_call(
        lambda *refs: x_kernel(fields, rows_local, *refs),
        grid=(rows_local // 16,),
        in_specs=specs,
        out_specs=[pl.BlockSpec((32, 128, 128), lambda i: (0, 0, 0))] * len(fields),
        out_shape=[jax.ShapeDtypeStruct((32, 128, 128), jnp.bfloat16)] * len(fields),
        scratch_shapes=[
            pltpu.VMEM((2, 32, 16, 128), jnp.float32),
            pltpu.VMEM((len(fields), 2048, 256), jnp.bfloat16),
            pltpu.VMEM((65 * PAD, 128), jnp.float32),
        ],
        compiler_params=pltpu.CompilerParams(vmem_limit_bytes=VMEM_LIMIT),
        cost_estimate=pl.CostEstimate(flops=2**30, bytes_accessed=2**22, transcendentals=0),
        name="lines_" + "_".join(fields),
    )(*[parts] * len(comps), x_matrix, x_twist, *after)


def meet_kernel(own, came, near, across, out):
    for b in range(out.shape[0]):
        for index, sign in ((0, -1.0), (1, 1.0)):
            rows, term_rows = slice(index * 64, index * 64 + 64), slice(64 - index * 64, 128 - index * 64)
            for half, (field, term) in enumerate(((own, near), (came, across))):
                value = field[b, rows, :].astype(jnp.float32) + sign * term[b, term_rows, :].astype(jnp.float32)
                at = index * 128 + half * 64
                out[b, at : at + 64, :] = value.astype(jnp.bfloat16)


def meet(own, came, near, across):
    return pl.pallas_call(
        meet_kernel,
        grid=(2,),
        in_specs=[pl.BlockSpec((16, 128, 128), lambda i: (i, 0, 0))] * 4,
        out_specs=pl.BlockSpec((16, 256, 128), lambda i: (i, 0, 0)),
        out_shape=jax.ShapeDtypeStruct((32, 256, 128), jnp.bfloat16),
        compiler_params=pltpu.CompilerParams(vmem_limit_bytes=VMEM_LIMIT),
        cost_estimate=pl.CostEstimate(flops=2**20, bytes_accessed=2**22, transcendentals=0),
        name="meet",
    )(own, came, near, across)


def y_lines(sources, twist, stage, lines):
    def one(part, carry):
        def load(c, d):
            source, first = sources[d // 32]
            return source[d % 32, pl.ds(first + c * 32 + part * 16, 16), :].astype(jnp.float32)

        for a in range(8):
            values = [(load(0, a + 8 * t), load(1, a + 8 * t)) for t in range(8)]
            for b, value in enumerate(dft8(values)):
                value = turned(value, a * b, 64)
                stage[0, b * 8 + a] = value[0]
                stage[1, b * 8 + a] = value[1]
        for b in range(8):
            for t, value in enumerate(dft8([(stage[0, b * 8 + a], stage[1, b * 8 + a]) for a in range(8)])):
                n = b + 8 * t
                c, s = twist[0, n : n + 1, :], twist[1, n : n + 1, :]
                at = pl.ds(n * 32 + part * 16, 16)
                lines[at, 0:128] = (value[0] * c - value[1] * s).astype(jnp.bfloat16)
                lines[at, 128:256] = (value[0] * s + value[1] * c).astype(jnp.bfloat16)
        return carry

    lax.fori_loop(0, 2, one, 0)


def y_squares(sources, matrix, twist, stage, lines, add):
    y_lines(sources, twist, stage, lines)
    for chunk in range(8):
        got = lax.dot_general(
            matrix[...], lines[pl.ds(chunk * 256, 256), :], NT, preferred_element_type=jnp.float32
        )
        got = got[0:128] + got[128:256]
        add((slice(None), slice(chunk * 256, chunk * 256 + 256)), got * got)


def y_first(own, came, matrix, twist, out, stage, lines):
    def add(at, square):
        out[at] = 1.0 + square

    y_squares(((own, 0), (came, 0)), matrix, twist, stage, lines, add)


def y_last(source, before, matrix, twist, out, stage, lines, total):
    def add(at, square):
        total[at] = before[at] + square

    def finish(at, square):
        total[at] = jnp.sqrt(total[at] + square)

    y_squares(((source, 0), (source, 64)), matrix, twist, stage, lines, add)
    y_squares(((source, 128), (source, 192)), matrix, twist, stage, lines, finish)

    def put(h, tile, value):
        value = value.astype(jnp.bfloat16)
        for c in range(4):
            for z in range(2):
                out[z * 4 + c, h * 16 : h * 16 + 16, tile * 128 : tile * 128 + 128] = value[c * 16 : c * 16 + 16]

    upper = (lax.broadcasted_iota(jnp.int32, (64, 128), 0) & 15) < 8
    for h in range(2):
        rows = slice(h * 64, h * 64 + 64)
        for tile in range(16):
            put(h, tile, total[rows, tile * 128 : tile * 128 + 128])
        before_first = pltpu.roll(total[rows, 15 * 128 : 16 * 128], 1, 0)
        after_last = pltpu.roll(total[rows, 0:128], 63, 0)
        put(h, 16, jnp.where(upper, before_first, after_last))


def y_transform(kernel, sources, y_matrix, y_twist):
    last = kernel is y_last
    sums = jax.ShapeDtypeStruct((128, 2048), jnp.float32)
    scratch = [pltpu.VMEM((2, 64, 16, 128), jnp.float32), pltpu.VMEM((2048, 256), jnp.bfloat16)]
    return pl.pallas_call(
        kernel,
        out_shape=jax.ShapeDtypeStruct((8, 32, 2176), jnp.bfloat16) if last else sums,
        scratch_shapes=scratch + ([pltpu.VMEM((128, 2048), jnp.float32)] if last else []),
        compiler_params=pltpu.CompilerParams(vmem_limit_bytes=VMEM_LIMIT),
        cost_estimate=pl.CostEstimate(flops=2**28, bytes_accessed=2**22, transcendentals=0),
        name=kernel.__name__,
    )(*sources, y_matrix, y_twist)


def smooth_coefficients():
    w = RELAX
    even = np.polynomial.polynomial.polypow([1 - 6 * w + 2 * w, w], 3)
    odd = np.polynomial.polynomial.polypow([1 - 6 * w - 2 * w, w], 3)
    return (even + odd) / 2, (even - odd) / 2


def brick_tile(field, source, h, tile):
    def held(index):
        start = index * 128 if isinstance(index, int) else pl.multiple_of(index * 128, 128)
        return field[source, h * 16 : h * 16 + 16, pl.ds(start, 128)].astype(jnp.float32)

    row = lax.broadcasted_iota(jnp.int32, (16, 128), 0)
    if isinstance(tile, int) and tile == 0:
        return jnp.where(row == 0, held(16), pltpu.roll(held(15), 1, 0))
    if isinstance(tile, int) and tile == 17:
        return jnp.where(row == 15, held(16), pltpu.roll(held(0), 15, 0))
    return held(tile - 1)


def regroup_kernel(field, own, other):
    me = lax.axis_index("gz")
    lane = lax.broadcasted_iota(jnp.int32, (16, 128), 1)

    def swapped(a, b, width):
        upper = (lane & width) != 0
        return (
            jnp.where(upper, pltpu.roll(b, width, 1), a),
            jnp.where(upper, b, pltpu.roll(a, 128 - width, 1)),
        )

    def regroup(z, target, tile):
        for ch in range(2):
            v = {
                (c, h): brick_tile(field, z * 4 + ch * 2 + c, h, tile)
                for c in range(2)
                for h in range(2)
            }
            p = {}
            for h in range(2):
                p[0, h], p[1, h] = swapped(v[0, h], v[1, h], 64)
            for y1 in range(2):
                s0, s1 = swapped(p[y1, 0], p[y1, 1], 16)
                y00, y01 = swapped(s0, s1, 32)
                target[tile * 4 + y1 * 2, :, ch * 128 : ch * 128 + 128] = y00
                target[tile * 4 + y1 * 2 + 1, :, ch * 128 : ch * 128 + 128] = y01

    def both(step, carry):
        for t in range(2):
            regroup(me, own, step * 2 + t + 1)
            regroup(1 - me, other, step * 2 + t + 1)
        return carry

    lax.fori_loop(0, 8, both, 0)
    for tile in (0, 17):
        regroup(me, own, tile)
        regroup(1 - me, other, tile)


def regroup(field):
    return pl.pallas_call(
        regroup_kernel,
        out_shape=[jax.ShapeDtypeStruct((72, 16, 256), jnp.float32)] * 2,
        compiler_params=pltpu.CompilerParams(vmem_limit_bytes=VMEM_LIMIT),
        cost_estimate=pl.CostEstimate(flops=2**24, bytes_accessed=2**23, transcendentals=0),
        name="regroup",
    )(field)


def edge_kernel(field, low, high):
    lane = lax.broadcasted_iota(jnp.int32, (16, 128), 1)
    for z in range(2):
        for group in range(5):
            last = first = jnp.zeros((16, 128), jnp.float32)
            for t in range(min(4, 18 - group * 4)):
                tile = group * 4 + t
                here = (lane & 24) == 8 * t
                last = jnp.where(here, pltpu.roll(brick_tile(field, z * 4 + 3, 1, tile), 100 + 8 * t, 1), last)
                first = jnp.where(here, pltpu.roll(brick_tile(field, z * 4, 0, tile), 4 + 8 * t, 1), first)
            low[z, :, group * 128 : group * 128 + 128] = last.astype(jnp.bfloat16)
            high[z, :, group * 128 : group * 128 + 128] = first.astype(jnp.bfloat16)


def edges(field):
    return pl.pallas_call(
        edge_kernel,
        out_shape=[jax.ShapeDtypeStruct((2, 16, 640), jnp.bfloat16)] * 2,
        compiler_params=pltpu.CompilerParams(vmem_limit_bytes=VMEM_LIMIT),
        name="edges",
    )(field)


def smooth_kernel(own, other, low, high, out, own_edge, other_edge, work, spread):
    own_c, other_c = [[float(v) for v in part] for part in smooth_coefficients()]
    me = lax.axis_index("gz")
    lane = lax.broadcasted_iota(jnp.int32, (16, 128), 1)
    is_low = (lane & 7) < 4

    def spread_edges(group, tiles):
        at = pl.ds(pl.multiple_of(group * 128, 128), 128)
        for z, target in ((me, own_edge), (1 - me, other_edge)):
            both = jnp.where(is_low, low[z, :, at].astype(jnp.float32), high[z, :, at].astype(jnp.float32))
            for t in range(tiles):
                for y in range(4):
                    target[(group * 4 + t) * 4 + y] = pltpu.roll(both, 124 - 32 * y - 8 * t, 1)

    def edge_group(group, carry):
        spread_edges(group, 4)
        return carry

    lax.fori_loop(0, 4, edge_group, 0)
    spread_edges(4, 2)

    def beside(ref, y, center):
        sides = pltpu.roll(center, 1, 1) + pltpu.roll(center, 383, 1)
        return sides + (ref(y - 1) + ref(y + 1))

    def own_at(y):
        return jnp.concatenate([own[y], own_edge[y]], axis=1)

    def other_at(y):
        return jnp.concatenate([other[y], other_edge[y]], axis=1)

    def each(begin, end, unroll, body):
        def some(step, carry):
            for t in range(unroll):
                body(begin + step * unroll + t)
            return carry

        lax.fori_loop(0, (end - begin) // unroll, some, 0)

    def first(y):
        center = own_at(y)
        work[0, y] = center * own_c[2] + other_at(y) * other_c[2] + beside(own_at, y, center) * own_c[3]

    def second(y):
        center = work[0, y]
        work[1, y] = own_at(y) * own_c[1] + other_at(y) * other_c[1] + beside(lambda i: work[0, i], y, center)

    def third(y):
        center = work[1, y]
        value = beside(lambda i: work[1, i], y, center)[:, 0:256]
        value = own[y] * own_c[0] + other[y] * other_c[0] + value
        for half in range(2):
            spread[pl.ds(half * 16 * PAD + y - 4, 16, stride=PAD), :] = value[:, half * 128 : half * 128 + 128]

    each(2, 70, 34, first)
    each(3, 69, 33, second)
    each(4, 68, 32, third)
    for half in range(2):
        for k in range(16):
            out[0, k * 64 : k * 64 + 64, half * 128 : half * 128 + 128] = spread[pl.ds((half * 16 + k) * PAD, 64), :]


def smooth(own, other, low, high):
    return pl.pallas_call(
        smooth_kernel,
        out_shape=jax.ShapeDtypeStruct((1, 1024, 256), jnp.float32),
        scratch_shapes=[
            pltpu.VMEM((72, 16, 128), jnp.float32),
            pltpu.VMEM((72, 16, 128), jnp.float32),
            pltpu.VMEM((2, 72, 16, 384), jnp.float32),
            pltpu.VMEM((33 * PAD, 128), jnp.float32),
        ],
        compiler_params=pltpu.CompilerParams(vmem_limit_bytes=VMEM_LIMIT),
        name="smooth",
    )(own, other, low, high)


def ring(value, axis, steps):
    count = lax.axis_size(axis)
    return lax.ppermute(value, axis, [(i, (i + steps) % count) for i in range(count)])


def between_y(value, target):
    pairs = []
    for y_hi in range(2):
        for gz in range(2):
            to_hi, to_gz = target(y_hi, gz)
            pairs.append((y_hi * 2 + gz, to_hi * 2 + to_gz))
    return lax.ppermute(value, ("yh", "gz"), pairs)


def shards(velocity_hat):
    x_matrix, x_twist, y_matrix, y_twist = tables()
    parts = velocity_hat.reshape((3, 2) + velocity_hat.shape[3:])

    def exchanged(array, axes):
        return lax.all_to_all(array, axes, split_axis=0, concat_axis=0, tiled=True)

    def lines(fields, after=()):
        return x_transform(fields, parts, x_matrix, x_twist, after)

    curl_own, curl_other = lines(("curl_x", "curl_y"))
    curl_z = lines(("curl_z",), (curl_own,))[0]
    term_own, term_other = lines(("u", "v"), (curl_z,))
    came = between_y(curl_other, lambda y_hi, gz: (1 - y_hi, gz))
    near = between_y(term_own, lambda y_hi, gz: (y_hi, 1 - gz))
    across = between_y(term_other, lambda y_hi, gz: (1 - y_hi, 1 - gz))
    line_2 = exchanged(curl_z, ("zc", "col"))
    came_2 = between_y(line_2[:, 64:], lambda y_hi, gz: (1 - y_hi, gz))
    both = exchanged(meet(curl_own, came, near, across), ("zc", "col"))
    squares = y_transform(y_first, (line_2, came_2), y_matrix, y_twist)
    magnitude = y_transform(y_last, (both, squares), y_matrix, y_twist)
    field = exchanged(magnitude, ("gz", "col"))
    last, first = edges(field)
    low, high = ring(last, ("yh", "zc"), 1), ring(first, ("yh", "zc"), -1)
    own, other = regroup(field)
    return smooth(own, other, low, high)


def solution(mesh):
    rows, cols, planes = mesh.devices.shape
    split = jax.sharding.Mesh(mesh.devices.reshape(2, rows // 2, cols, planes), ("yh", "zc", "col", "gz"))
    return jax.shard_map(
        shards,
        mesh=split,
        in_specs=(P(None, None, "gz", ("yh", "zc", "col"), None),),
        out_specs=P("gz", "col", ("yh", "zc")),
        check_vma=False,
    )
```
